32 devices in a mesh: member: 2 (over y), node: 4 (over z), feat: 4 (over x, core).
Axes of the slice: x: 2, y: 2, z: 4, core: 2. Of those that a mesh axis runs over, the one named last changes fastest.
Arguments:
- features: bfloat16 [32768, 1024], P(('member', 'node'), 'feat'), parts along dimension 0, may hold values from -6 to 6
- w_self: bfloat16 [2048, 1024], P(('member', 'node')), parts along dimension 0, may hold values from -0.125 to 0.125
- w_neigh: bfloat16 [2048, 1024], P(('member', 'node')), parts along dimension 0, may hold values from -0.125 to 0.125
- bias: float32 [2048], P('member'), parts along dimension 0, may hold values from -3 to 3
- dst_ids: int32 [4096], P('node'), may hold values from 0 to 4095, as said below
- send_blocks: int32 [4, 4, 2], P('node'), may hold values from 0 to 31, as said below
- tile_info: int32 [4, 3, 64], P('node'), may hold values from 0 to 256, as said below
- tile_edges: int32 [4, 64, 256], P('node'), may hold values from 0 to 16383, as said below
- tile_counts: int32 [4], P('node'), may hold values from 48 to 64, as said below
- cotangent: bfloat16 [8192, 1024], P(('member', 'node', 'feat')), parts along dimension 0, may hold values from -6 to 6
Outputs:
- layer_out: bfloat16 [8192, 1024], P(('member', 'node', 'feat')), parts along dimension 0
- grad_features: bfloat16 [32768, 1024], P(('member', 'node'), 'feat'), parts along dimension 0
The draws below stay inside these ranges and needn't reach their ends.
There are 2 independent parts, one for each index of `member`. The reference program is written for one: setup_inputs(seed, part) draws one part's arguments, and reference() takes and returns one part's arrays. A program takes and returns all parts, laid end to end along the dimension named above; an argument that names none is the same for every part. Nothing has to cross between parts.
Inputs may be any that keep to these rules, and one draw needn't show every extreme that they name: `dst_ids`: entries 1024 * m to 1024 * (m + 1) - 1 belong to node shard m and are distinct rows of it. send_blocks[p, m, s] is a block of shard p; the 2 entries of one pair (p, m) are distinct. tile_info[m, 0, t] is a slot below 8, tile_info[m, 1, t] a destination block below 8, tile_info[m, 2, t] an edge count from 1 to 256; every shard has a tile with 256 edges. `tile_edges`: only the first tile_info[m, 2, t] entries of a tile count; in every destination block some rows receive no edge from any tile. `tile_counts`: some shard uses all 64 tiles.
All inputs are finite; a program needn't handle non-finite values.
Results may differ from the reference program's by a relative error of at most 0.0054.
Values may be sent and summed in bfloat16 or wider, within the bound.
A program may use at most 64 MiB of HBM per device.

```python
import jax
import jax.numpy as jnp
from jax import lax

D = 1024
H = 1024
TB = 128
BLK_DEV = 32
DST_BLK = 8
SLOT_CAP = 2
EDGES_T = 256
ROWS_DEV = 4096
DST_DEV = 1024
TILE_CAP = 64
SLOTS = 8
NODES = 16384
DSTS = 4096
N_NODE = 4


def graph_tables(key):
    k_slot, k_block, k_edge, k_full, k_source, k_pick, k_perm, k_cover = jax.random.split(key, 8)
    random_slots = jax.random.randint(k_slot, (N_NODE, TILE_CAP), 0, SLOT_CAP * N_NODE)
    cover_keys = jax.random.split(k_cover, N_NODE)
    covers = jax.vmap(lambda sub_key: jax.random.permutation(sub_key, SLOTS))(cover_keys)
    tile_pos = jnp.arange(TILE_CAP)
    cover_pick = covers[:, jnp.minimum(tile_pos, SLOTS - 1)]
    slot_ids = jnp.where(tile_pos[None, :] < SLOTS, cover_pick, random_slots)
    block_ids = jax.random.randint(k_block, (N_NODE, TILE_CAP), 0, DST_BLK)
    edge_total = jax.random.randint(k_edge, (N_NODE, TILE_CAP), 1, EDGES_T + 1)
    fullest = jax.random.randint(k_full, (N_NODE, 1), 0, TILE_CAP)
    edge_total = jnp.where(tile_pos[None, :] == fullest, EDGES_T, edge_total)
    table = jnp.stack([slot_ids, block_ids, edge_total], axis=1).astype(jnp.int32)
    spare_rows = max(1, TB // 16)
    perm_keys = jax.random.split(k_perm, N_NODE * DST_BLK)
    orders = jax.vmap(lambda sub_key: jax.random.permutation(sub_key, TB))(perm_keys)
    orders = orders.reshape(N_NODE, DST_BLK, TB)
    tile_orders = jnp.take_along_axis(orders, jnp.broadcast_to(block_ids[:, :, None], (N_NODE, TILE_CAP, TB)), axis=1)
    pick_index = jax.random.randint(k_pick, (N_NODE, TILE_CAP, EDGES_T), 0, TB - spare_rows)
    target_row = jnp.take_along_axis(tile_orders, pick_index, axis=2)
    source_row = jax.random.randint(k_source, (N_NODE, TILE_CAP, EDGES_T), 0, TB)
    return (table, (source_row * TB + target_row).astype(jnp.int32))


def draw_tile_info(key, part):
    return graph_tables(key)[0]


def draw_tile_edges(key, part):
    return graph_tables(key)[1]


def draw_send_blocks(key, part):
    key = jax.random.fold_in(key, 11)
    perm_keys = jax.random.split(key, N_NODE * N_NODE)
    orders = jax.vmap(lambda sub_key: jax.random.permutation(sub_key, BLK_DEV)[:SLOT_CAP])(perm_keys)
    return orders.reshape(N_NODE, N_NODE, SLOT_CAP).astype(jnp.int32)


def draw_dst_ids(key, part):
    key = jax.random.fold_in(key, 12)
    perm_keys = jax.random.split(key, N_NODE)
    orders = jax.vmap(lambda sub_key: jax.random.permutation(sub_key, ROWS_DEV)[:DST_DEV])(perm_keys)
    return orders.reshape(-1).astype(jnp.int32)


def draw_tile_counts(key, part):
    key = jax.random.fold_in(key, 13)
    k_count, k_full = jax.random.split(key)
    live_tiles = jax.random.randint(k_count, (N_NODE,), max(1, 3 * TILE_CAP // 4), TILE_CAP + 1)
    fullest = jax.random.randint(k_full, (), 0, N_NODE)
    return jnp.where(jnp.arange(N_NODE) == fullest, TILE_CAP, live_tiles).astype(jnp.int32)


def steps_of(own_key, dims, shards, low, top_value):
    gain, own = 1.0, jax.random.fold_in(own_key, 6)
    for position, parts in shards:
        draws = jnp.exp(jax.random.uniform(jax.random.fold_in(own, position), (parts,), jnp.float32, low / len(shards), top_value / len(shards)))
        gain = gain * jnp.repeat(draws, dims[position] // parts).reshape([-1 if axis == position else 1 for axis in range(len(dims))])
    return gain


def bell_draw(rng, extent, scale, limit, cuts=(), kind=jnp.bfloat16):
    level = steps_of(rng, extent, cuts, -0.22, 0.18) if cuts else 1.0
    result = jax.random.normal(rng, extent, jnp.float32) * scale * level
    return jnp.minimum(jnp.maximum(result, -limit), limit).astype(kind)


def setup_inputs(seed: int = 0, part: int = 0) -> dict:
    key_list = jax.random.split(jax.random.key(seed), 11)
    part_splits = jax.random.split(jax.random.fold_in(key_list[10], part), 11)
    return {
        "features": bell_draw(part_splits[0], (NODES, D), 1.0, 6.0, ((0, 4), (1, 4))),
        "w_self": bell_draw(part_splits[1], (D, H), (2 * D) ** -0.5, 0.125, ((0, 4),)),
        "w_neigh": bell_draw(part_splits[2], (D, H), (2 * D) ** -0.5, 0.125, ((0, 4),)),
        "bias": bell_draw(part_splits[3], (H,), 0.5, 3.0, (), jnp.float32),
        "dst_ids": draw_dst_ids(jax.random.fold_in(key_list[10], 71), part),
        "send_blocks": draw_send_blocks(jax.random.fold_in(key_list[10], 71), part),
        "tile_info": draw_tile_info(jax.random.fold_in(key_list[10], 71), part),
        "tile_edges": draw_tile_edges(jax.random.fold_in(key_list[10], 71), part),
        "tile_counts": draw_tile_counts(jax.random.fold_in(key_list[10], 71), part),
        "cotangent": bell_draw(part_splits[9], (DSTS, H), 1.0, 6.0, ((0, 16),)),
    }


def tile_matrices(edge_codes, edge_total, live_mask):
    tile_index = jnp.arange(TILE_CAP)[:, None]
    valid_edge = (jnp.arange(EDGES_T)[None, :] < edge_total[:, None]) & live_mask[:, None]
    source_row = edge_codes // TB
    target_row = edge_codes % TB
    empty = jnp.zeros((TILE_CAP, TB, TB), jnp.float32)
    return empty.at[tile_index, target_row, source_row].add(valid_edge.astype(jnp.float32))


def reference(features, w_self, w_neigh, bias, dst_ids, send_blocks, tile_info, tile_edges, tile_counts, cotangent):
    block_view = features.reshape(N_NODE, BLK_DEV, TB, D)
    shard_rows = features.reshape(N_NODE, ROWS_DEV, D)
    shard_ids = dst_ids.reshape(N_NODE, DST_DEV)
    shard_cot = cotangent.reshape(N_NODE, DST_DEV, H)
    peer_ids = jnp.arange(N_NODE)

    def shard_pass(grad_rows, shard_index):
        chosen = send_blocks[:, shard_index, :]
        received = block_view[peer_ids[:, None], chosen].reshape(SLOTS, TB, D)
        table = tile_info[shard_index]
        live_mask = jnp.arange(TILE_CAP) < tile_counts[shard_index]
        adjacency = tile_matrices(tile_edges[shard_index], table[2], live_mask)
        degree = jax.ops.segment_sum(jnp.sum(adjacency, axis=2), table[1], DST_BLK)
        row_scale = jnp.maximum(degree, 1.0)
        products = jnp.einsum('tds,tsf->tdf', adjacency, received[table[0]].astype(jnp.float32))
        agg_sum = jax.ops.segment_sum(products, table[1], DST_BLK)
        mean_rows = (agg_sum / row_scale[:, :, None]).astype(jnp.bfloat16).reshape(DST_DEV, D)
        own_rows = shard_rows[shard_index][shard_ids[shard_index]]
        pre_act = jnp.dot(own_rows, w_self, preferred_element_type=jnp.float32)
        pre_act = pre_act + jnp.dot(mean_rows, w_neigh, preferred_element_type=jnp.float32) + bias
        sig_gate = jax.nn.sigmoid(pre_act)
        layer_out = (pre_act * sig_gate).astype(jnp.bfloat16)
        cot_rows = shard_cot[shard_index].astype(jnp.float32)
        grad_pre = (cot_rows * sig_gate * (1.0 + pre_act * (1.0 - sig_gate))).astype(jnp.bfloat16)
        grad_own = jnp.dot(grad_pre, w_self.T, preferred_element_type=jnp.float32).astype(jnp.bfloat16)
        grad_agg = jnp.dot(grad_pre, w_neigh.T, preferred_element_type=jnp.float32).astype(jnp.bfloat16)
        grad_sum = (grad_agg.astype(jnp.float32).reshape(DST_BLK, TB, D) / row_scale[:, :, None]).astype(jnp.bfloat16)
        back_terms = jnp.einsum('tds,tdf->tsf', adjacency, grad_sum[table[1]].astype(jnp.float32))
        grad_slot = jax.ops.segment_sum(back_terms, table[0], SLOTS).astype(jnp.bfloat16)
        targets = (peer_ids[:, None] * BLK_DEV + chosen).reshape(-1)
        grad_rows = grad_rows.at[targets].add(grad_slot.astype(jnp.float32))
        flat_rows = grad_rows.reshape(NODES, D)
        flat_rows = flat_rows.at[shard_index * ROWS_DEV + shard_ids[shard_index]].add(grad_own.astype(jnp.float32))
        return flat_rows.reshape(N_NODE * BLK_DEV, TB, D), layer_out

    start_grads = jnp.zeros((N_NODE * BLK_DEV, TB, D), jnp.float32)
    grad_rows, outputs = lax.scan(shard_pass, start_grads, jnp.arange(N_NODE))
    return outputs.reshape(DSTS, H), grad_rows.reshape(NODES, D).astype(jnp.bfloat16)
```

```python
import functools
import math

import jax
import jax.numpy as jnp
from jax import lax
from jax.experimental import pallas as pl
from jax.experimental.pallas import tpu as pltpu
from jax.sharding import PartitionSpec as P

TB = 128
VMEM_BYTES = 60 * 1024 * 1024
F32 = jnp.float32
BF16 = jnp.bfloat16
VMEM = pl.BlockSpec(memory_space=pltpu.VMEM)
SMEM = pl.BlockSpec(memory_space=pltpu.SMEM)
ANY = pl.BlockSpec(memory_space=pl.ANY)


def dot_nn(left, right):
    return lax.dot_general(left, right, (((1,), (0,)), ((), ())), preferred_element_type=F32)


def dot_nt(left, right):
    return lax.dot_general(left, right, (((1,), (1,)), ((), ())), preferred_element_type=F32)


def prep_kernel(
    group, counts, info, send, edges, features, adj_ref, scale_ref, out_blocks, sums, sems
):
    n_dst, n_slot = sums.shape[0], sums.shape[1]
    node_count, per_node = send.shape
    copies = []
    for peer in range(node_count):
        for s in range(per_node):
            q = peer * per_node + s
            row = pl.multiple_of(send[peer, s] * TB, TB)
            copies.append(
                pltpu.make_async_copy(
                    features.at[pl.ds(row, TB), :],
                    out_blocks.at[pl.ds(q * TB, TB), :],
                    sems.at[q],
                )
            )
    for copy in copies:
        copy.start()
    edge_slots = edges.shape[1]
    live = counts[0]

    def zero(b, _):
        sums[b] = jnp.zeros(sums.shape[1:], F32)
        return 0

    lax.fori_loop(0, n_dst, zero, 0)
    sub = lax.broadcasted_iota(jnp.int32, (TB, edge_slots), 0)
    lane = lax.broadcasted_iota(jnp.int32, (1, edge_slots), 1)

    def step(i, _):
        parts = []
        for k in range(group):
            t = i * group + k
            codes = edges[pl.ds(t, 1), :]
            total = jnp.where(t < live, info[2, t], 0)
            source = codes // TB
            target = jnp.where(lane < total, codes % TB, -1)
            t_hot = jnp.where(sub == target, 1.0, 0.0).astype(BF16)
            s_hot = jnp.where(sub == source, 1.0, 0.0).astype(BF16)
            parts.append((t, dot_nt(t_hot, s_hot)))
        for t, part in parts:
            sums[info[1, t], info[0, t]] += part
        return 0

    lax.fori_loop(0, (live + group - 1) // group, step, 0)

    def finish(b, _):
        rows = pl.ds(pl.multiple_of(b * TB, TB), TB)
        total = jnp.zeros((TB, TB), F32)
        for s in range(n_slot):
            block = sums[b, s]
            total = total + block
            adj_ref[rows, s * TB : (s + 1) * TB] = block.astype(BF16)
        degree = jnp.sum(total, axis=1, keepdims=True)
        scale_ref[rows, :] = jnp.broadcast_to(jnp.maximum(degree, 1.0), (TB, TB))
        return 0

    lax.fori_loop(0, n_dst, finish, 0)
    for copy in copies:
        copy.wait()


def main_kernel(
    cfg,
    out_blocks,
    w_self,
    w_neigh,
    bias,
    adj,
    scale,
    features,
    id_col,
    id_row,
    back_row,
    cot,
    layer_ref,
    grad_ref,
    wbuf,
    adj_t,
    recv,
    own,
    mean,
    gath,
    g_own,
    g_sum,
    slot_out,
    ret,
    total,
    sbufs,
    rbufs,
    accs,
    f_send,
    f_recv,
    w_right,
    w_left,
    w_recv,
    r_send,
    r_recv,
    g_send,
    g_recv,
    b_send,
    b_recv,
):
    N, F, C, relay, WC = cfg
    L = F.bit_length() - 1
    node = lax.axis_index("node")
    feat = lax.axis_index("feat")
    bits = [(feat // (1 << j)) % 2 for j in range(L)]
    partner = [feat + (1 - 2 * bits[j]) * (1 << j) for j in range(L)]
    rows_all, cw = own.shape
    H = bias.shape[1]
    R = rows_all // F
    RC = R // C
    per = out_blocks.shape[0] // N

    def remote(src, dst, ss, rs, axis, index):
        return pltpu.make_async_remote_copy(
            src_ref=src,
            dst_ref=dst,
            send_sem=ss,
            recv_sem=rs,
            device_id={axis: index},
            device_id_type=pl.DeviceIdType.MESH,
        )

    barrier = pltpu.get_barrier_semaphore()
    for d in range(1, N):
        pl.semaphore_signal(
            barrier, inc=1, device_id={"node": (node + d) % N}, device_id_type=pl.DeviceIdType.MESH
        )
    for j in range(L):
        pl.semaphore_signal(
            barrier, inc=1, device_id={"feat": partner[j]}, device_id_type=pl.DeviceIdType.MESH
        )
    pl.semaphore_wait(barrier, N - 1 + L)

    def node_rows(index):
        return pl.ds(pl.multiple_of(index * per, per), per)

    def exchange(src, dst, ss, rs, d):
        peer = (node + d) % N
        return remote(
            src.at[node_rows(peer), :], dst.at[node_rows(node), :], ss.at[d], rs.at[d], "node", peer
        )

    for d in range(1, N):
        exchange(out_blocks, recv, f_send, f_recv, d).start()
    recv[node_rows(node), :] = out_blocks[node_rows(node), :]

    piece = cw // WC

    def w_copy(c, sem, peer):
        part = wbuf.at[c // WC, pl.ds(pl.multiple_of((c % WC) * piece, piece), piece), :]
        return remote(part, part, sem.at[c], w_recv.at[c], "node", peer)

    go_right = (node >= feat) & (node < N - 1)
    go_left = (node <= feat) & (node > 0)
    up, down = (node + 1) % N, (node + N - 1) % N

    if relay:

        @pl.when(node == feat)
        def _():
            wbuf[0] = w_self[...]
            wbuf[1] = w_neigh[...]
    else:
        wbuf[0] = w_self[...]
        wbuf[1] = w_neigh[...]

    feat_rows = features.shape[0]
    GC = 2 * WC
    own_step = rows_all // GC
    row_lane = lax.broadcasted_iota(jnp.int32, (own_step, feat_rows), 1)

    def load(c, _):
        if relay:

            @pl.when(node != feat)
            def _():
                w_copy(c, w_right, up).wait_recv()

            @pl.when(go_right)
            def _():
                w_copy(c, w_right, up).start()

            @pl.when(go_left)
            def _():
                w_copy(c, w_left, down).start()

        rows = pl.ds(pl.multiple_of(c * own_step, own_step), own_step)
        hot = jnp.where(row_lane == id_col[rows, :], 1.0, 0.0).astype(BF16)
        own[rows, :] = dot_nn(hot, features[...]).astype(BF16)
        adj_t[:, rows] = adj[rows, :].T
        return 0

    lax.fori_loop(0, GC, load, 0)

    for d in range(1, N):
        exchange(out_blocks, recv, f_send, f_recv, d).wait_recv()

    def aggregate(i, _):
        rows = pl.ds(pl.multiple_of(i * TB, TB), TB)
        value = dot_nn(adj[rows, :], recv[...]) / scale[rows, :1]
        mean[rows, :] = value.astype(BF16)
        return 0

    lax.fori_loop(0, rows_all // TB, aggregate, 0)

    def partial(g, c):
        rows = pl.ds(pl.multiple_of(g * R + c * RC, RC), RC)
        return dot_nn(own[rows, :], wbuf[0]) + dot_nn(mean[rows, :], wbuf[1])

    def r_copy(j, i, c):
        index = sum((F >> (k + 1)) * C for k in range(j)) + i * C + c
        return remote(
            sbufs[j].at[i, c],
            rbufs[j].at[i, c],
            r_send.at[index],
            r_recv.at[index],
            "feat",
            partner[j],
        )

    for c in range(C):
        for i in range(F // 2):
            sbufs[0][i, c] = partial(2 * i + 1 - bits[0], c).astype(BF16)
            r_copy(0, i, c).start()
    for c in range(C):
        for i in range(F // 2):
            accs[0][i, c] = partial(2 * i + bits[0], c)
    for j in range(1, L):
        for c in range(C):
            for a in range(F >> (j + 1)):
                for i in (2 * a, 2 * a + 1):
                    r_copy(j - 1, i, c).wait_recv()
                i = 2 * a + 1 - bits[j]
                sbufs[j][a, c] = (accs[j - 1][i, c] + rbufs[j - 1][i, c].astype(F32)).astype(BF16)
                r_copy(j, a, c).start()
                i = 2 * a + bits[j]
                accs[j][a, c] = accs[j - 1][i, c] + rbufs[j - 1][i, c].astype(F32)

    def g_copy(j, k, c, block):
        index = (j * F + k) * C + c
        part = gath.at[block, c]
        return remote(part, part, g_send.at[index], g_recv.at[index], "feat", partner[j])

    def block_of(mask):
        index = feat
        for j in range(L):
            if mask >> j & 1:
                index = index + (1 - 2 * bits[j]) * (1 << j)
        return index

    def backward(block, c):
        rows = pl.ds(pl.multiple_of(block * R + c * RC, RC), RC)
        rows_grad = gath[block, c]
        g_own[rows, :] = dot_nt(rows_grad, wbuf[0]).astype(BF16)
        to_mean = dot_nt(rows_grad, wbuf[1]).astype(BF16).astype(F32)
        g_sum[rows, :] = (to_mean / scale[rows, :1]).astype(BF16)

    for c in range(C):
        r_copy(L - 1, 0, c).wait_recv()
        pre = accs[L - 1][0, c] + rbufs[L - 1][0, c].astype(F32) + bias[...]
        sig = jax.nn.sigmoid(pre)
        rows = pl.ds(c * RC, RC)
        layer_ref[rows, :] = (pre * sig).astype(BF16)
        gath[feat, c] = (cot[rows, :].astype(F32) * sig * (1.0 + pre * (1.0 - sig))).astype(BF16)
        for j in reversed(range(L)):
            g_copy(j, 0, c, feat).start()
    for c in range(C):
        backward(feat, c)
    for c in range(C):
        for mask in sorted(range(1, F), key=lambda m: (bin(m).count("1"), m)):
            j = (mask & -mask).bit_length() - 1
            g_copy(j, mask >> (j + 1), c, block_of(mask)).wait_recv()
            for low in range(j):
                g_copy(low, mask >> (low + 1), c, block_of(mask)).start()
            backward(block_of(mask), c)

    def slot_grad(peer):
        rows = node_rows(peer)
        slot_out[rows, :] = dot_nn(adj_t[rows, :], g_sum[...]).astype(BF16)

    for d in range(1, N):
        slot_grad((node + d) % N)
        exchange(slot_out, ret, b_send, b_recv, d).start()
    slot_grad(node)
    ret[node_rows(node), :] = slot_out[node_rows(node), :]

    dst_lane = lax.broadcasted_iota(jnp.int32, (TB, rows_all), 0)

    def scatter_own(b, _):
        rows = pl.ds(pl.multiple_of(b * TB, TB), TB)
        hot = jnp.where(dst_lane + b * TB == id_row[...], 1.0, 0.0).astype(BF16)
        total[rows, :] = dot_nn(hot, g_own[...])
        return 0

    lax.fori_loop(0, feat_rows // TB, scatter_own, 0)
    for d in range(1, N):
        exchange(slot_out, ret, b_send, b_recv, d).wait_recv()
    slot_lane = lax.broadcasted_iota(jnp.int32, (TB, ret.shape[0]), 0)

    def scatter_back(b, _):
        rows = pl.ds(pl.multiple_of(b * TB, TB), TB)
        hot = jnp.where(slot_lane + b * TB == back_row[...], 1.0, 0.0).astype(BF16)
        grad_ref[rows, :] = (total[rows, :] + dot_nn(hot, ret[...])).astype(BF16)
        return 0

    lax.fori_loop(0, feat_rows // TB, scatter_back, 0)

    for d in range(1, N):
        exchange(out_blocks, recv, f_send, f_recv, d).wait_send()
        exchange(slot_out, ret, b_send, b_recv, d).wait_send()
    for j in range(L):
        for c in range(C):
            for i in range(F >> (j + 1)):
                r_copy(j, i, c).wait_send()
            for k in range(F >> (j + 1)):
                g_copy(j, k, c, block_of(k << (j + 1))).wait_send()
    if relay:

        def drain(c, _):
            @pl.when(go_right)
            def _():
                w_copy(c, w_right, up).wait_send()

            @pl.when(go_left)
            def _():
                w_copy(c, w_left, down).wait_send()

            return 0

        lax.fori_loop(0, GC, drain, 0)


def on_device(
    features,
    w_self,
    w_neigh,
    bias,
    dst_ids,
    send_blocks,
    tile_info,
    tile_edges,
    tile_counts,
    cotangent,
):
    N = lax.axis_size("node")
    F = lax.axis_size("feat")
    L = F.bit_length() - 1
    feat_rows, cw = features.shape
    rows_all = dst_ids.shape[0]
    H = bias.shape[0]
    R = rows_all // F
    C = 2
    WC = 4
    per_node = send_blocks.shape[2]
    slots = N * per_node
    slot_rows = slots * TB
    n_dst = rows_all // TB
    chosen = send_blocks[0]
    capacity = tile_edges.shape[1]

    adj, scale, out_blocks = pl.pallas_call(
        functools.partial(prep_kernel, math.gcd(capacity, 4)),
        out_shape=(
            jax.ShapeDtypeStruct((rows_all, slot_rows), BF16),
            jax.ShapeDtypeStruct((rows_all, TB), F32),
            jax.ShapeDtypeStruct((slot_rows, cw), BF16),
        ),
        in_specs=[SMEM, SMEM, SMEM, VMEM, ANY],
        out_specs=(VMEM, VMEM, ANY),
        scratch_shapes=[
            pltpu.VMEM((n_dst, slots, TB, TB), F32),
            pltpu.SemaphoreType.DMA((slots,)),
        ],
        compiler_params=pltpu.CompilerParams(vmem_limit_bytes=VMEM_BYTES),
        name="prep",
    )(tile_counts, tile_info[0], chosen, tile_edges[0], features)

    relay = N == F and w_self.shape[0] == cw
    if not relay:
        offset = lax.axis_index("feat") * cw
        w_self, w_neigh = (
            lax.dynamic_slice_in_dim(
                lax.all_gather(w, "node", axis=0, tiled=True), offset, cw, 0
            )
            for w in (w_self, w_neigh)
        )
    back_ids = (chosen.reshape(-1, 1) * TB + jnp.arange(TB)[None, :]).reshape(1, -1)
    dma = pltpu.SemaphoreType.DMA
    halves = [F >> (j + 1) for j in range(L)]
    layer_out, grad_rows = pl.pallas_call(
        functools.partial(main_kernel, (N, F, C, relay, WC)),
        out_shape=(
            jax.ShapeDtypeStruct((R, H), BF16),
            jax.ShapeDtypeStruct((feat_rows, cw), BF16),
        ),
        in_specs=[VMEM] * 11,
        out_specs=(VMEM, VMEM),
        scratch_shapes=[
            pltpu.VMEM((2, cw, H), BF16),
            pltpu.VMEM((slot_rows, rows_all), BF16),
            pltpu.VMEM((slot_rows, cw), BF16),
            pltpu.VMEM((rows_all, cw), BF16),
            pltpu.VMEM((rows_all, cw), BF16),
            pltpu.VMEM((F, C, R // C, H), BF16),
            pltpu.VMEM((rows_all, cw), BF16),
            pltpu.VMEM((rows_all, cw), BF16),
            pltpu.VMEM((slot_rows, cw), BF16),
            pltpu.VMEM((slot_rows, cw), BF16),
            pltpu.VMEM((feat_rows, cw), F32),
            [pltpu.VMEM((h, C, R // C, H), BF16) for h in halves],
            [pltpu.VMEM((h, C, R // C, H), BF16) for h in halves],
            [pltpu.VMEM((h, C, R // C, H), F32) for h in halves],
            dma((N,)),
            dma((N,)),
            dma((2 * WC,)),
            dma((2 * WC,)),
            dma((2 * WC,)),
            dma((F * C,)),
            dma((F * C,)),
            dma((L * F * C,)),
            dma((L * F * C,)),
            dma((N,)),
            dma((N,)),
        ],
        compiler_params=pltpu.CompilerParams(
            collective_id=0, has_side_effects=True, vmem_limit_bytes=VMEM_BYTES
        ),
        name="layer",
    )(
        out_blocks,
        w_self,
        w_neigh,
        bias.reshape(1, H),
        adj,
        scale,
        features,
        dst_ids.reshape(-1, 1),
        dst_ids.reshape(1, -1),
        back_ids,
        cotangent,
    )
    return (layer_out, grad_rows)


def solution(mesh):
    return jax.shard_map(
        on_device,
        mesh=mesh,
        in_specs=(
            P(("member", "node"), "feat"),
            P(("member", "node"), None),
            P(("member", "node"), None),
            P("member"),
            P("node"),
            P("node", None, None),
            P("node", None, None),
            P("node", None, None),
            P("node"),
            P(("member", "node", "feat"), None),
        ),
        out_specs=(P(("member", "node", "feat"), None), P(("member", "node"), "feat")),
        check_vma=False,
    )
```

```python
import functools
import math

import jax
import jax.numpy as jnp
from jax import lax
from jax.experimental import pallas as pl
from jax.experimental.pallas import tpu as pltpu
from jax.sharding import PartitionSpec as P

TB = 128
VMEM_BYTES = 60 * 1024 * 1024
F32 = jnp.float32
BF16 = jnp.bfloat16
VMEM = pl.BlockSpec(memory_space=pltpu.VMEM)
SMEM = pl.BlockSpec(memory_space=pltpu.SMEM)
ANY = pl.BlockSpec(memory_space=pl.ANY)


def dot_nn(left, right):
    return lax.dot_general(left, right, (((1,), (0,)), ((), ())), preferred_element_type=F32)


def dot_nt(left, right):
    return lax.dot_general(left, right, (((1,), (1,)), ((), ())), preferred_element_type=F32)


def plan_kernel(n_slot, counts, send, info, edges, features, src_ref, dst_ref, bound_ref, out_blocks, sems):
    per_node, node_count = send.shape
    copies = []
    for peer in range(node_count):
        for s in range(per_node):
            q = peer * per_node + s
            row = pl.multiple_of(send[s, peer] * TB, TB)
            copies.append(
                pltpu.make_async_copy(
                    features.at[pl.ds(row, TB), :],
                    out_blocks.at[pl.ds(q * TB, TB), :],
                    sems.at[q],
                )
            )
    for copy in copies:
        copy.start()
    capacity, edge_slots = edges.shape
    live = counts[0]
    width = bound_ref.shape[1]
    tile = lax.broadcasted_iota(jnp.int32, (1, capacity), 1)
    key = jnp.where(tile < live, info[1] * n_slot + info[0], width).astype(F32)
    total = jnp.where(tile < live, info[2], 0).astype(F32)
    lane = lax.broadcasted_iota(jnp.int32, (capacity, capacity), 1)
    sub = lax.broadcasted_iota(jnp.int32, (capacity, capacity), 0)
    diag = lane == sub

    def column(row):
        return jnp.sum(jnp.where(diag, jnp.broadcast_to(row, diag.shape), 0.0), axis=1, keepdims=True)

    key_col = column(key)
    before = (key_col < key) | ((key_col == key) & (sub < lane))
    rank = jnp.sum(jnp.where(before, 1.0, 0.0), axis=0, keepdims=True)
    order = jnp.where(sub.astype(F32) == rank, 1.0, 0.0).astype(BF16)
    slot_lane = lax.broadcasted_iota(jnp.int32, (capacity, width), 1).astype(F32)
    bound = jnp.sum(jnp.where(key_col < slot_lane, 1.0, 0.0), axis=0, keepdims=True)
    bound_ref[...] = bound.astype(jnp.int32)
    codes = edges[...]
    place = lax.broadcasted_iota(jnp.int32, (capacity, edge_slots), 1).astype(F32)
    source = (codes // TB).astype(F32)
    target = jnp.where(place < column(total), (codes % TB).astype(F32), -1.0)
    src_ref[...] = dot_nn(order, source.astype(BF16))
    dst_ref[...] = dot_nn(order, target.astype(BF16))
    for copy in copies:
        copy.wait()


def final_kernel(send, base, back, layer, grad_ref, layer_ref, rows_sum):
    per_node, node_count = send.shape
    step = pl.program_id(0)
    layer_ref[...] = layer[...]
    rows_sum[...] = base[...].astype(F32)
    blocks = rows_sum.shape[0] // TB
    for peer in range(node_count):
        for s in range(per_node):
            q = peer * per_node + s
            local = send[s, peer] - step * blocks

            @pl.when((local >= 0) & (local < blocks))
            def _():
                rows = pl.ds(pl.multiple_of(local * TB, TB), TB)
                rows_sum[rows, :] += back[q * TB : (q + 1) * TB, :].astype(F32)

    grad_ref[...] = rows_sum[...].astype(BF16)


def main_kernel(
    cfg,
    out_blocks,
    w_self,
    w_neigh,
    bias,
    src_of,
    dst_of,
    bounds,
    features,
    id_row,
    cot,
    layer_ref,
    ret,
    base_ref,
    wbuf,
    prefix,
    adj,
    adj_t,
    scale,
    recv,
    own,
    mean,
    gath,
    g_own,
    g_sum,
    slot_out,
    total,
    sbufs,
    rbufs,
    accs,
    f_send,
    f_recv,
    w_right,
    w_left,
    w_recv,
    r_send,
    r_recv,
    g_send,
    g_recv,
    b_send,
    b_recv,
    out_sem,
):
    N, F, C, relay, WC = cfg
    L = F.bit_length() - 1
    node = lax.axis_index("node")
    feat = lax.axis_index("feat")
    bits = [(feat // (1 << j)) % 2 for j in range(L)]
    partner = [feat + (1 - 2 * bits[j]) * (1 << j) for j in range(L)]
    rows_all, cw = own.shape
    H = bias.shape[1]
    R = rows_all // F
    RC = R // C
    per = out_blocks.shape[0] // N

    def remote(src, dst, ss, rs, axis, index):
        return pltpu.make_async_remote_copy(
            src_ref=src,
            dst_ref=dst,
            send_sem=ss,
            recv_sem=rs,
            device_id={axis: index},
            device_id_type=pl.DeviceIdType.MESH,
        )

    barrier = pltpu.get_barrier_semaphore()
    for d in range(1, N):
        pl.semaphore_signal(
            barrier, inc=1, device_id={"node": (node + d) % N}, device_id_type=pl.DeviceIdType.MESH
        )
    for j in range(L):
        pl.semaphore_signal(
            barrier, inc=1, device_id={"feat": partner[j]}, device_id_type=pl.DeviceIdType.MESH
        )
    pl.semaphore_wait(barrier, N - 1 + L)

    def node_rows(index):
        return pl.ds(pl.multiple_of(index * per, per), per)

    def exchange(src, dst, ss, rs, d):
        peer = (node + d) % N
        return remote(
            src.at[node_rows(peer), :], dst.at[node_rows(node), :], ss.at[d], rs.at[d], "node", peer
        )

    for d in range(1, N):
        exchange(out_blocks, recv, f_send, f_recv, d).start()
    recv[node_rows(node), :] = out_blocks[node_rows(node), :]

    piece = cw // WC

    def w_copy(c, sem, peer):
        part = wbuf.at[c // WC, pl.ds(pl.multiple_of((c % WC) * piece, piece), piece), :]
        return remote(part, part, sem.at[c], w_recv.at[c], "node", peer)

    go_right = (node >= feat) & (node < N - 1)
    go_left = (node <= feat) & (node > 0)
    up, down = (node + 1) % N, (node + N - 1) % N

    if relay:

        @pl.when(node == feat)
        def _():
            wbuf[0] = w_self[...]
            wbuf[1] = w_neigh[...]
    else:
        wbuf[0] = w_self[...]
        wbuf[1] = w_neigh[...]

    feat_rows = features.shape[0]
    GC = 2 * WC
    own_step = rows_all // GC
    capacity, edge_slots = src_of.shape
    n_dst = rows_all // TB
    n_slot = recv.shape[0] // TB
    group = capacity // GC
    sub_f = lax.broadcasted_iota(jnp.int32, (TB, edge_slots), 0).astype(BF16)
    one, nil = jnp.ones((), BF16), jnp.zeros((), BF16)
    lane_id = lax.broadcasted_iota(jnp.int32, (TB, TB), 1)
    prefix[0] = jnp.zeros((TB, TB), F32)

    def load(c, _):
        running = prefix[c * group]
        for k in range(group):
            t = c * group + k
            source = jnp.broadcast_to(src_of[pl.ds(t, 1), :].astype(BF16), sub_f.shape)
            target = jnp.broadcast_to(dst_of[pl.ds(t, 1), :].astype(BF16), sub_f.shape)
            t_hot = jnp.where(sub_f == target, one, nil)
            s_hot = jnp.where(sub_f == source, one, nil)
            running = running + dot_nt(t_hot, s_hot)
            prefix[t + 1] = running
        for k in range(own_step // TB):
            rows = pl.ds(pl.multiple_of(c * own_step + k * TB, TB), TB)
            ids = jnp.broadcast_to(id_row[:, rows].astype(F32), (TB, TB)).T.astype(jnp.int32)
            hot = jnp.concatenate(
                [
                    jnp.where(lane_id + b * TB == ids, 1.0, 0.0).astype(BF16)
                    for b in range(feat_rows // TB)
                ],
                axis=1,
            )
            own[rows, :] = dot_nn(hot, features[...]).astype(BF16)
        if relay:

            @pl.when(node != feat)
            def _():
                w_copy(c, w_right, up).wait_recv()

            @pl.when(go_right)
            def _():
                w_copy(c, w_right, up).start()

            @pl.when(go_left)
            def _():
                w_copy(c, w_left, down).start()

        return 0

    lax.fori_loop(0, GC, load, 0)

    def assemble(b, _):
        rows = pl.ds(pl.multiple_of(b * TB, TB), TB)
        degree = jnp.zeros((TB, TB), F32)
        for s in range(n_slot):
            low, high = bounds[0, b * n_slot + s], bounds[0, b * n_slot + s + 1]
            block = prefix[high] - prefix[low]
            degree = degree + block
            adj[rows, s * TB : (s + 1) * TB] = block.astype(BF16)
            adj_t[s * TB : (s + 1) * TB, rows] = block.T.astype(BF16)
        degree = jnp.sum(degree, axis=1, keepdims=True)
        scale[rows, :] = jnp.broadcast_to(jnp.maximum(degree, 1.0), (TB, TB))
        return 0

    lax.fori_loop(0, n_dst, assemble, 0)

    for d in range(1, N):
        exchange(out_blocks, recv, f_send, f_recv, d).wait_recv()

    def aggregate(i, _):
        rows = pl.ds(pl.multiple_of(i * TB, TB), TB)
        value = dot_nn(adj[rows, :], recv[...]) / scale[rows, :1]
        mean[rows, :] = value.astype(BF16)
        return 0

    lax.fori_loop(0, rows_all // TB, aggregate, 0)

    def partial(g, c):
        rows = pl.ds(pl.multiple_of(g * R + c * RC, RC), RC)
        return dot_nn(own[rows, :], wbuf[0]) + dot_nn(mean[rows, :], wbuf[1])

    def r_copy(j, i, c):
        index = sum((F >> (k + 1)) * C for k in range(j)) + i * C + c
        return remote(
            sbufs[j].at[i, c],
            rbufs[j].at[i, c],
            r_send.at[index],
            r_recv.at[index],
            "feat",
            partner[j],
        )

    for c in range(C):
        for i in range(F // 2):
            sbufs[0][i, c] = partial(2 * i + 1 - bits[0], c).astype(BF16)
            r_copy(0, i, c).start()
    for c in range(C):
        for i in range(F // 2):
            accs[0][i, c] = partial(2 * i + bits[0], c)
    for j in range(1, L):
        for c in range(C):
            for a in range(F >> (j + 1)):
                for i in (2 * a, 2 * a + 1):
                    r_copy(j - 1, i, c).wait_recv()
                i = 2 * a + 1 - bits[j]
                sbufs[j][a, c] = (accs[j - 1][i, c] + rbufs[j - 1][i, c].astype(F32)).astype(BF16)
                r_copy(j, a, c).start()
                i = 2 * a + bits[j]
                accs[j][a, c] = accs[j - 1][i, c] + rbufs[j - 1][i, c].astype(F32)

    def g_copy(j, k, c, block):
        index = (j * F + k) * C + c
        part = gath.at[block, c]
        return remote(part, part, g_send.at[index], g_recv.at[index], "feat", partner[j])

    def block_of(mask):
        index = feat
        for j in range(L):
            if mask >> j & 1:
                index = index + (1 - 2 * bits[j]) * (1 << j)
        return index

    def backward(block, c):
        rows = pl.ds(pl.multiple_of(block * R + c * RC, RC), RC)
        rows_grad = gath[block, c]
        g_own[rows, :] = dot_nt(rows_grad, wbuf[0]).astype(BF16)
        to_mean = dot_nt(rows_grad, wbuf[1]).astype(BF16).astype(F32)
        g_sum[rows, :] = (to_mean / scale[rows, :1]).astype(BF16)

    for c in range(C):
        r_copy(L - 1, 0, c).wait_recv()
        pre = accs[L - 1][0, c] + rbufs[L - 1][0, c].astype(F32) + bias[...]
        sig = jax.nn.sigmoid(pre)
        rows = pl.ds(c * RC, RC)
        layer_ref[rows, :] = (pre * sig).astype(BF16)
        gath[feat, c] = (cot[rows, :].astype(F32) * sig * (1.0 + pre * (1.0 - sig))).astype(BF16)
        for j in reversed(range(L)):
            g_copy(j, 0, c, feat).start()
    for c in range(C):
        backward(feat, c)
    for c in range(C):
        for mask in sorted(range(1, F), key=lambda m: (bin(m).count("1"), m)):
            j = (mask & -mask).bit_length() - 1
            g_copy(j, mask >> (j + 1), c, block_of(mask)).wait_recv()
            for low in range(j):
                g_copy(low, mask >> (low + 1), c, block_of(mask)).start()
            backward(block_of(mask), c)

    def slot_grad(peer):
        rows = node_rows(peer)
        slot_out[rows, :] = dot_nn(adj_t[rows, :], g_sum[...]).astype(BF16)

    for d in range(1, N):
        slot_grad((node + d) % N)
        exchange(slot_out, ret, b_send, b_recv, d).start()
    slot_grad(node)
    ret[node_rows(node), :] = slot_out[node_rows(node), :]

    dst_lane = lax.broadcasted_iota(jnp.int32, (TB, rows_all), 0)

    def scatter_own(b, _):
        rows = pl.ds(pl.multiple_of(b * TB, TB), TB)
        hot = jnp.where(dst_lane + b * TB == id_row[...], 1.0, 0.0).astype(BF16)
        total[rows, :] = dot_nn(hot, g_own[...]).astype(BF16)
        return 0

    quarter = feat_rows // 4

    def put(k):
        rows = pl.ds(k * quarter, quarter)
        return pltpu.make_async_copy(total.at[rows, :], base_ref.at[rows, :], out_sem.at[k])

    for k in range(4):
        lax.fori_loop(k * quarter // TB, (k + 1) * quarter // TB, scatter_own, 0)
        put(k).start()
    for d in range(1, N):
        exchange(slot_out, ret, b_send, b_recv, d).wait_recv()
    for k in range(4):
        put(k).wait()

    for d in range(1, N):
        exchange(out_blocks, recv, f_send, f_recv, d).wait_send()
        exchange(slot_out, ret, b_send, b_recv, d).wait_send()
    for j in range(L):
        for c in range(C):
            for i in range(F >> (j + 1)):
                r_copy(j, i, c).wait_send()
            for k in range(F >> (j + 1)):
                g_copy(j, k, c, block_of(k << (j + 1))).wait_send()
    if relay:

        def drain(c, _):
            @pl.when(go_right)
            def _():
                w_copy(c, w_right, up).wait_send()

            @pl.when(go_left)
            def _():
                w_copy(c, w_left, down).wait_send()

            return 0

        lax.fori_loop(0, GC, drain, 0)


def on_device(
    features,
    w_self,
    w_neigh,
    bias,
    dst_ids,
    send_blocks,
    tile_info,
    tile_edges,
    tile_counts,
    cotangent,
):
    N = lax.axis_size("node")
    F = lax.axis_size("feat")
    L = F.bit_length() - 1
    feat_rows, cw = features.shape
    rows_all = dst_ids.shape[0]
    H = bias.shape[0]
    R = rows_all // F
    C = 2
    WC = 4
    per_node = send_blocks.shape[2]
    slots = N * per_node
    slot_rows = slots * TB
    n_dst = rows_all // TB
    capacity = tile_edges.shape[1]

    send = jnp.swapaxes(send_blocks, 1, 2)[0]
    info = jnp.swapaxes(tile_info, 0, 1)
    width = -(-(n_dst * slots + 1) // TB) * TB
    src_of, dst_of, bounds, out_blocks = pl.pallas_call(
        functools.partial(plan_kernel, slots),
        out_shape=(
            jax.ShapeDtypeStruct(tile_edges.shape[1:], F32),
            jax.ShapeDtypeStruct(tile_edges.shape[1:], F32),
            jax.ShapeDtypeStruct((1, width), jnp.int32),
            jax.ShapeDtypeStruct((slot_rows, cw), BF16),
        ),
        in_specs=[SMEM, SMEM, VMEM, VMEM, ANY],
        out_specs=(VMEM, VMEM, VMEM, VMEM),
        scratch_shapes=[pltpu.SemaphoreType.DMA((slots,))],
        compiler_params=pltpu.CompilerParams(vmem_limit_bytes=VMEM_BYTES),
        name="plan",
    )(tile_counts, send, info, tile_edges[0], features)

    relay = N == F and w_self.shape[0] == cw
    if not relay:
        offset = lax.axis_index("feat") * cw
        w_self, w_neigh = (
            lax.dynamic_slice_in_dim(
                lax.all_gather(w, "node", axis=0, tiled=True), offset, cw, 0
            )
            for w in (w_self, w_neigh)
        )
    dma = pltpu.SemaphoreType.DMA
    halves = [F >> (j + 1) for j in range(L)]
    layer_rows, back, base = pl.pallas_call(
        functools.partial(main_kernel, (N, F, C, relay, WC)),
        out_shape=(
            jax.ShapeDtypeStruct((R, H), BF16),
            jax.ShapeDtypeStruct((slot_rows, cw), BF16),
            jax.ShapeDtypeStruct((feat_rows, cw), BF16),
        ),
        in_specs=[VMEM] * 6 + [SMEM] + [VMEM] * 3,
        out_specs=(VMEM, VMEM, ANY),
        scratch_shapes=[
            pltpu.VMEM((2, cw, H), BF16),
            pltpu.VMEM((capacity + 1, TB, TB), F32),
            pltpu.VMEM((rows_all, slot_rows), BF16),
            pltpu.VMEM((slot_rows, rows_all), BF16),
            pltpu.VMEM((rows_all, TB), F32),
            pltpu.VMEM((slot_rows, cw), BF16),
            pltpu.VMEM((rows_all, cw), BF16),
            pltpu.VMEM((rows_all, cw), BF16),
            pltpu.VMEM((F, C, R // C, H), BF16),
            pltpu.VMEM((rows_all, cw), BF16),
            pltpu.VMEM((rows_all, cw), BF16),
            pltpu.VMEM((slot_rows, cw), BF16),
            pltpu.VMEM((feat_rows, cw), BF16),
            [pltpu.VMEM((h, C, R // C, H), BF16) for h in halves],
            [pltpu.VMEM((h, C, R // C, H), BF16) for h in halves],
            [pltpu.VMEM((h, C, R // C, H), F32) for h in halves],
            dma((N,)),
            dma((N,)),
            dma((2 * WC,)),
            dma((2 * WC,)),
            dma((2 * WC,)),
            dma((F * C,)),
            dma((F * C,)),
            dma((L * F * C,)),
            dma((L * F * C,)),
            dma((N,)),
            dma((N,)),
            dma((4,)),
        ],
        compiler_params=pltpu.CompilerParams(
            collective_id=0, has_side_effects=True, vmem_limit_bytes=VMEM_BYTES
        ),
        name="layer",
    )(
        out_blocks,
        w_self,
        w_neigh,
        bias.reshape(1, H),
        src_of,
        dst_of,
        bounds,
        features,
        dst_ids.reshape(1, -1),
        cotangent,
    )
    steps = math.gcd(math.gcd(feat_rows // TB, R // 16), 8)
    grad_rows, layer_out = pl.pallas_call(
        final_kernel,
        grid=(steps,),
        out_shape=(
            jax.ShapeDtypeStruct((feat_rows, cw), BF16),
            jax.ShapeDtypeStruct((R, H), BF16),
        ),
        in_specs=[
            SMEM,
            pl.BlockSpec((feat_rows // steps, cw), lambda i: (i, 0)),
            pl.BlockSpec((slot_rows, cw), lambda i: (0, 0)),
            pl.BlockSpec((R // steps, H), lambda i: (i, 0)),
        ],
        out_specs=(
            pl.BlockSpec((feat_rows // steps, cw), lambda i: (i, 0)),
            pl.BlockSpec((R // steps, H), lambda i: (i, 0)),
        ),
        scratch_shapes=[pltpu.VMEM((feat_rows // steps, cw), F32)],
        compiler_params=pltpu.CompilerParams(vmem_limit_bytes=VMEM_BYTES),
        name="finish",
    )(send, base, back, layer_rows)
    return (layer_out, grad_rows)


def solution(mesh):
    return jax.shard_map(
        on_device,
        mesh=mesh,
        in_specs=(
            P(("member", "node"), "feat"),
            P(("member", "node"), None),
            P(("member", "node"), None),
            P("member"),
            P("node"),
            P("node", None, None),
            P("node", None, None),
            P("node", None, None),
            P("node"),
            P(("member", "node", "feat"), None),
        ),
        out_specs=(P(("member", "node", "feat"), None), P(("member", "node"), "feat")),
        check_vma=False,
    )
```

```python
import functools
import math

import jax
import jax.numpy as jnp
from jax import lax
from jax.experimental import pallas as pl
from jax.experimental.pallas import tpu as pltpu
from jax.sharding import PartitionSpec as P

TB = 128
VMEM_BYTES = 60 * 1024 * 1024
F32 = jnp.float32
BF16 = jnp.bfloat16
VMEM = pl.BlockSpec(memory_space=pltpu.VMEM)
SMEM = pl.BlockSpec(memory_space=pltpu.SMEM)
ANY = pl.BlockSpec(memory_space=pl.ANY)


def dot_nn(left, right):
    return lax.dot_general(left, right, (((1,), (0,)), ((), ())), preferred_element_type=F32)


def dot_nt(left, right):
    return lax.dot_general(left, right, (((1,), (1,)), ((), ())), preferred_element_type=F32)


def plan_kernel(n_slot, counts, send, info, edges, features, src_ref, dst_ref, bound_ref, out_blocks, sems):
    per_node, node_count = send.shape
    copies = []
    for peer in range(node_count):
        for s in range(per_node):
            q = peer * per_node + s
            row = pl.multiple_of(send[s, peer] * TB, TB)
            copies.append(
                pltpu.make_async_copy(
                    features.at[pl.ds(row, TB), :],
                    out_blocks.at[pl.ds(q * TB, TB), :],
                    sems.at[q],
                )
            )
    for copy in copies:
        copy.start()
    capacity, edge_slots = edges.shape
    live = counts[0]
    width = bound_ref.shape[1]
    tile = lax.broadcasted_iota(jnp.int32, (1, capacity), 1)
    key = jnp.where(tile < live, info[1] * n_slot + info[0], width).astype(F32)
    total = jnp.where(tile < live, info[2], 0).astype(F32)
    lane = lax.broadcasted_iota(jnp.int32, (capacity, capacity), 1)
    sub = lax.broadcasted_iota(jnp.int32, (capacity, capacity), 0)
    diag = lane == sub

    def column(row):
        return jnp.sum(jnp.where(diag, jnp.broadcast_to(row, diag.shape), 0.0), axis=1, keepdims=True)

    key_col = column(key)
    before = (key_col < key) | ((key_col == key) & (sub < lane))
    rank = jnp.sum(jnp.where(before, 1.0, 0.0), axis=0, keepdims=True)
    order = jnp.where(sub.astype(F32) == rank, 1.0, 0.0).astype(BF16)
    slot_lane = lax.broadcasted_iota(jnp.int32, (capacity, width), 1).astype(F32)
    bound = jnp.sum(jnp.where(key_col < slot_lane, 1.0, 0.0), axis=0, keepdims=True)
    bound_ref[...] = bound.astype(jnp.int32)
    codes = edges[...]
    place = lax.broadcasted_iota(jnp.int32, (capacity, edge_slots), 1).astype(F32)
    source = (codes // TB).astype(F32)
    target = jnp.where(place < column(total), (codes % TB).astype(F32), -1.0)
    src_ref[...] = dot_nn(order, source.astype(BF16))
    dst_ref[...] = dot_nn(order, target.astype(BF16))
    for copy in copies:
        copy.wait()


def final_kernel(send, base, back, layer, grad_ref, layer_ref, rows_sum):
    per_node, node_count = send.shape
    step = pl.program_id(0)
    layer_ref[...] = layer[...]
    rows_sum[...] = base[...].astype(F32)
    blocks = rows_sum.shape[0] // TB
    for peer in range(node_count):
        for s in range(per_node):
            q = peer * per_node + s
            local = send[s, peer] - step * blocks

            @pl.when((local >= 0) & (local < blocks))
            def _():
                rows = pl.ds(pl.multiple_of(local * TB, TB), TB)
                rows_sum[rows, :] += back[q * TB : (q + 1) * TB, :].astype(F32)

    grad_ref[...] = rows_sum[...].astype(BF16)


def main_kernel(
    cfg,
    out_blocks,
    w_self,
    w_neigh,
    bias,
    src_of,
    dst_of,
    bounds,
    features,
    id_row,
    cot,
    layer_ref,
    ret,
    base_ref,
    wbuf,
    wvia,
    prefix,
    adj,
    adj_t,
    scale,
    recv,
    own,
    mean,
    gath,
    g_own,
    g_sum,
    slot_out,
    total,
    sbufs,
    rbufs,
    accs,
    f_send,
    f_recv,
    w_send,
    w_recv,
    h_send,
    h_recv,
    r_send,
    r_recv,
    g_send,
    g_recv,
    b_send,
    b_recv,
    out_sem,
):
    N, F, C, relay, WC = cfg
    L = F.bit_length() - 1
    node = lax.axis_index("node")
    feat = lax.axis_index("feat")
    bits = [(feat // (1 << j)) % 2 for j in range(L)]
    partner = [feat + (1 - 2 * bits[j]) * (1 << j) for j in range(L)]
    rows_all, cw = own.shape
    H = bias.shape[1]
    R = rows_all // F
    RC = R // C
    per = out_blocks.shape[0] // N

    def remote(src, dst, ss, rs, axis, index):
        return pltpu.make_async_remote_copy(
            src_ref=src,
            dst_ref=dst,
            send_sem=ss,
            recv_sem=rs,
            device_id={axis: index},
            device_id_type=pl.DeviceIdType.MESH,
        )

    barrier = pltpu.get_barrier_semaphore()
    for d in range(1, N):
        pl.semaphore_signal(
            barrier, inc=1, device_id={"node": (node + d) % N}, device_id_type=pl.DeviceIdType.MESH
        )
    for j in range(L):
        pl.semaphore_signal(
            barrier, inc=1, device_id={"feat": partner[j]}, device_id_type=pl.DeviceIdType.MESH
        )
    pl.semaphore_wait(barrier, N - 1 + L)

    def node_rows(index):
        return pl.ds(pl.multiple_of(index * per, per), per)

    def exchange(src, dst, ss, rs, d):
        peer = (node + d) % N
        return remote(
            src.at[node_rows(peer), :], dst.at[node_rows(node), :], ss.at[d], rs.at[d], "node", peer
        )

    for d in range(1, N):
        exchange(out_blocks, recv, f_send, f_recv, d).start()
    recv[node_rows(node), :] = out_blocks[node_rows(node), :]

    GC = 2 * WC
    piece = cw // GC
    across = partner[L - 1]
    up, down = (node + 1) % N, (node + N - 1) % N

    def w_rows(c):
        return pl.ds(pl.multiple_of(c * piece, piece), piece)

    def w_copy(c, way, side, peer):
        part = (wbuf.at[0] if way == 0 else wvia).at[w_rows(c), :]
        return remote(part, part, w_send.at[way, side, c], w_recv.at[way, c], "node", peer)

    def hop_copy(c):
        return remote(
            wvia.at[w_rows(c), :], wbuf.at[1, w_rows(c), :], h_send.at[c], h_recv.at[c], "feat", across
        )

    roots = (feat, across)
    go_right = [(node >= r) & (node < N - 1) for r in roots]
    go_left = [(node <= r) & (node > 0) for r in roots]

    if relay:

        @pl.when(node == feat)
        def _():
            wbuf[0] = w_self[...]
            wbuf[1] = w_neigh[...]

        @pl.when(node == across)
        def _():
            wvia[...] = w_neigh[...]
    else:
        wbuf[0] = w_self[...]
        wbuf[1] = w_neigh[...]

    feat_rows = features.shape[0]
    own_step = rows_all // GC
    capacity, edge_slots = src_of.shape
    n_dst = rows_all // TB
    n_slot = recv.shape[0] // TB
    group = capacity // GC
    sub_f = lax.broadcasted_iota(jnp.int32, (TB, edge_slots), 0).astype(BF16)
    one, nil = jnp.ones((), BF16), jnp.zeros((), BF16)
    lane_id = lax.broadcasted_iota(jnp.int32, (TB, TB), 1)
    prefix[0] = jnp.zeros((TB, TB), F32)

    def load(c, _):
        running = prefix[c * group]
        for k in range(group):
            t = c * group + k
            source = jnp.broadcast_to(src_of[pl.ds(t, 1), :].astype(BF16), sub_f.shape)
            target = jnp.broadcast_to(dst_of[pl.ds(t, 1), :].astype(BF16), sub_f.shape)
            t_hot = jnp.where(sub_f == target, one, nil)
            s_hot = jnp.where(sub_f == source, one, nil)
            running = running + dot_nt(t_hot, s_hot)
            prefix[t + 1] = running
        for k in range(own_step // TB):
            rows = pl.ds(pl.multiple_of(c * own_step + k * TB, TB), TB)
            ids = jnp.broadcast_to(id_row[:, rows].astype(F32), (TB, TB)).T.astype(jnp.int32)
            hot = jnp.concatenate(
                [
                    jnp.where(lane_id + b * TB == ids, 1.0, 0.0).astype(BF16)
                    for b in range(feat_rows // TB)
                ],
                axis=1,
            )
            own[rows, :] = dot_nn(hot, features[...]).astype(BF16)
        if relay:

            for way in range(2):

                @pl.when(node != roots[way])
                def _():
                    w_copy(c, way, 0, up).wait_recv()

                @pl.when(go_right[way])
                def _():
                    w_copy(c, way, 0, up).start()

                @pl.when(go_left[way])
                def _():
                    w_copy(c, way, 1, down).start()

            @pl.when(node != across)
            def _():
                hop_copy(c).start()

        return 0

    lax.fori_loop(0, GC, load, 0)

    def assemble(b, _):
        rows = pl.ds(pl.multiple_of(b * TB, TB), TB)
        degree = jnp.zeros((TB, TB), F32)
        for s in range(n_slot):
            low, high = bounds[0, b * n_slot + s], bounds[0, b * n_slot + s + 1]
            block = prefix[high] - prefix[low]
            degree = degree + block
            adj[rows, s * TB : (s + 1) * TB] = block.astype(BF16)
            adj_t[s * TB : (s + 1) * TB, rows] = block.T.astype(BF16)
        degree = jnp.sum(degree, axis=1, keepdims=True)
        scale[rows, :] = jnp.broadcast_to(jnp.maximum(degree, 1.0), (TB, TB))
        return 0

    lax.fori_loop(0, n_dst, assemble, 0)

    for d in range(1, N):
        exchange(out_blocks, recv, f_send, f_recv, d).wait_recv()

    def aggregate(i, _):
        rows = pl.ds(pl.multiple_of(i * TB, TB), TB)
        value = dot_nn(adj[rows, :], recv[...]) / scale[rows, :1]
        mean[rows, :] = value.astype(BF16)
        return 0

    lax.fori_loop(0, rows_all // TB, aggregate, 0)

    if relay:

        @pl.when(node != feat)
        def _():
            def landed(c, _):
                hop_copy(c).wait_recv()
                return 0

            lax.fori_loop(0, GC, landed, 0)

    def partial(g, c):
        rows = pl.ds(pl.multiple_of(g * R + c * RC, RC), RC)
        return dot_nn(own[rows, :], wbuf[0]) + dot_nn(mean[rows, :], wbuf[1])

    def r_copy(j, i, c):
        index = sum((F >> (k + 1)) * C for k in range(j)) + i * C + c
        return remote(
            sbufs[j].at[i, c],
            rbufs[j].at[i, c],
            r_send.at[index],
            r_recv.at[index],
            "feat",
            partner[j],
        )

    for c in range(C):
        for i in range(F // 2):
            sbufs[0][i, c] = partial(2 * i + 1 - bits[0], c).astype(BF16)
            r_copy(0, i, c).start()
    for c in range(C):
        for i in range(F // 2):
            accs[0][i, c] = partial(2 * i + bits[0], c)
    for j in range(1, L):
        for c in range(C):
            for a in range(F >> (j + 1)):
                for i in (2 * a, 2 * a + 1):
                    r_copy(j - 1, i, c).wait_recv()
                i = 2 * a + 1 - bits[j]
                sbufs[j][a, c] = (accs[j - 1][i, c] + rbufs[j - 1][i, c].astype(F32)).astype(BF16)
                r_copy(j, a, c).start()
                i = 2 * a + bits[j]
                accs[j][a, c] = accs[j - 1][i, c] + rbufs[j - 1][i, c].astype(F32)

    def g_copy(j, k, c, block):
        index = (j * F + k) * C + c
        part = gath.at[block, c]
        return remote(part, part, g_send.at[index], g_recv.at[index], "feat", partner[j])

    def block_of(mask):
        index = feat
        for j in range(L):
            if mask >> j & 1:
                index = index + (1 - 2 * bits[j]) * (1 << j)
        return index

    def backward(block, c):
        rows = pl.ds(pl.multiple_of(block * R + c * RC, RC), RC)
        rows_grad = gath[block, c]
        g_own[rows, :] = dot_nt(rows_grad, wbuf[0]).astype(BF16)
        to_mean = dot_nt(rows_grad, wbuf[1]).astype(BF16).astype(F32)
        g_sum[rows, :] = (to_mean / scale[rows, :1]).astype(BF16)

    for c in range(C):
        r_copy(L - 1, 0, c).wait_recv()
        pre = accs[L - 1][0, c] + rbufs[L - 1][0, c].astype(F32) + bias[...]
        sig = jax.nn.sigmoid(pre)
        rows = pl.ds(c * RC, RC)
        layer_ref[rows, :] = (pre * sig).astype(BF16)
        gath[feat, c] = (cot[rows, :].astype(F32) * sig * (1.0 + pre * (1.0 - sig))).astype(BF16)
        for j in reversed(range(L)):
            g_copy(j, 0, c, feat).start()
    for c in range(C):
        backward(feat, c)
    for c in range(C):
        for mask in sorted(range(1, F), key=lambda m: (bin(m).count("1"), m)):
            j = (mask & -mask).bit_length() - 1
            g_copy(j, mask >> (j + 1), c, block_of(mask)).wait_recv()
            for low in range(j):
                g_copy(low, mask >> (low + 1), c, block_of(mask)).start()
            backward(block_of(mask), c)

    def slot_grad(peer):
        rows = node_rows(peer)
        slot_out[rows, :] = dot_nn(adj_t[rows, :], g_sum[...]).astype(BF16)

    for d in range(1, N):
        slot_grad((node + d) % N)
        exchange(slot_out, ret, b_send, b_recv, d).start()
    slot_grad(node)
    ret[node_rows(node), :] = slot_out[node_rows(node), :]

    dst_lane = lax.broadcasted_iota(jnp.int32, (TB, rows_all), 0)

    def scatter_own(b, _):
        rows = pl.ds(pl.multiple_of(b * TB, TB), TB)
        hot = jnp.where(dst_lane + b * TB == id_row[...], 1.0, 0.0).astype(BF16)
        total[rows, :] = dot_nn(hot, g_own[...]).astype(BF16)
        return 0

    quarter = feat_rows // 4

    def put(k):
        rows = pl.ds(k * quarter, quarter)
        return pltpu.make_async_copy(total.at[rows, :], base_ref.at[rows, :], out_sem.at[k])

    for k in range(4):
        lax.fori_loop(k * quarter // TB, (k + 1) * quarter // TB, scatter_own, 0)
        put(k).start()
    for d in range(1, N):
        exchange(slot_out, ret, b_send, b_recv, d).wait_recv()
    for k in range(4):
        put(k).wait()

    for d in range(1, N):
        exchange(out_blocks, recv, f_send, f_recv, d).wait_send()
        exchange(slot_out, ret, b_send, b_recv, d).wait_send()
    for j in range(L):
        for c in range(C):
            for i in range(F >> (j + 1)):
                r_copy(j, i, c).wait_send()
            for k in range(F >> (j + 1)):
                g_copy(j, k, c, block_of(k << (j + 1))).wait_send()
    if relay:

        def drain(c, _):
            for way in range(2):

                @pl.when(go_right[way])
                def _():
                    w_copy(c, way, 0, up).wait_send()

                @pl.when(go_left[way])
                def _():
                    w_copy(c, way, 1, down).wait_send()

            @pl.when(node != across)
            def _():
                hop_copy(c).wait_send()

            return 0

        lax.fori_loop(0, GC, drain, 0)


def on_device(
    features,
    w_self,
    w_neigh,
    bias,
    dst_ids,
    send_blocks,
    tile_info,
    tile_edges,
    tile_counts,
    cotangent,
):
    N = lax.axis_size("node")
    F = lax.axis_size("feat")
    L = F.bit_length() - 1
    feat_rows, cw = features.shape
    rows_all = dst_ids.shape[0]
    H = bias.shape[0]
    R = rows_all // F
    C = 2
    WC = 4
    per_node = send_blocks.shape[2]
    slots = N * per_node
    slot_rows = slots * TB
    n_dst = rows_all // TB
    capacity = tile_edges.shape[1]

    send = jnp.swapaxes(send_blocks, 1, 2)[0]
    info = jnp.swapaxes(tile_info, 0, 1)
    width = -(-(n_dst * slots + 1) // TB) * TB
    src_of, dst_of, bounds, out_blocks = pl.pallas_call(
        functools.partial(plan_kernel, slots),
        out_shape=(
            jax.ShapeDtypeStruct(tile_edges.shape[1:], F32),
            jax.ShapeDtypeStruct(tile_edges.shape[1:], F32),
            jax.ShapeDtypeStruct((1, width), jnp.int32),
            jax.ShapeDtypeStruct((slot_rows, cw), BF16),
        ),
        in_specs=[SMEM, SMEM, VMEM, VMEM, ANY],
        out_specs=(VMEM, VMEM, VMEM, VMEM),
        scratch_shapes=[pltpu.SemaphoreType.DMA((slots,))],
        compiler_params=pltpu.CompilerParams(vmem_limit_bytes=VMEM_BYTES),
        name="plan",
    )(tile_counts, send, info, tile_edges[0], features)

    relay = N == F and w_self.shape[0] == cw
    if not relay:
        offset = lax.axis_index("feat") * cw
        w_self, w_neigh = (
            lax.dynamic_slice_in_dim(
                lax.all_gather(w, "node", axis=0, tiled=True), offset, cw, 0
            )
            for w in (w_self, w_neigh)
        )
    dma = pltpu.SemaphoreType.DMA
    halves = [F >> (j + 1) for j in range(L)]
    layer_rows, back, base = pl.pallas_call(
        functools.partial(main_kernel, (N, F, C, relay, WC)),
        out_shape=(
            jax.ShapeDtypeStruct((R, H), BF16),
            jax.ShapeDtypeStruct((slot_rows, cw), BF16),
            jax.ShapeDtypeStruct((feat_rows, cw), BF16),
        ),
        in_specs=[VMEM] * 6 + [SMEM] + [VMEM] * 3,
        out_specs=(VMEM, VMEM, ANY),
        scratch_shapes=[
            pltpu.VMEM((2, cw, H), BF16),
            pltpu.VMEM((cw, H), BF16),
            pltpu.VMEM((capacity + 1, TB, TB), F32),
            pltpu.VMEM((rows_all, slot_rows), BF16),
            pltpu.VMEM((slot_rows, rows_all), BF16),
            pltpu.VMEM((rows_all, TB), F32),
            pltpu.VMEM((slot_rows, cw), BF16),
            pltpu.VMEM((rows_all, cw), BF16),
            pltpu.VMEM((rows_all, cw), BF16),
            pltpu.VMEM((F, C, R // C, H), BF16),
            pltpu.VMEM((rows_all, cw), BF16),
            pltpu.VMEM((rows_all, cw), BF16),
            pltpu.VMEM((slot_rows, cw), BF16),
            pltpu.VMEM((feat_rows, cw), BF16),
            [pltpu.VMEM((h, C, R // C, H), BF16) for h in halves],
            [pltpu.VMEM((h, C, R // C, H), BF16) for h in halves],
            [pltpu.VMEM((h, C, R // C, H), F32) for h in halves],
            dma((N,)),
            dma((N,)),
            dma((2, 2, 2 * WC)),
            dma((2, 2 * WC)),
            dma((2 * WC,)),
            dma((2 * WC,)),
            dma((F * C,)),
            dma((F * C,)),
            dma((L * F * C,)),
            dma((L * F * C,)),
            dma((N,)),
            dma((N,)),
            dma((4,)),
        ],
        compiler_params=pltpu.CompilerParams(
            collective_id=0, has_side_effects=True, vmem_limit_bytes=VMEM_BYTES
        ),
        name="layer",
    )(
        out_blocks,
        w_self,
        w_neigh,
        bias.reshape(1, H),
        src_of,
        dst_of,
        bounds,
        features,
        dst_ids.reshape(1, -1),
        cotangent,
    )
    steps = math.gcd(math.gcd(feat_rows // TB, R // 16), 8)
    grad_rows, layer_out = pl.pallas_call(
        final_kernel,
        grid=(steps,),
        out_shape=(
            jax.ShapeDtypeStruct((feat_rows, cw), BF16),
            jax.ShapeDtypeStruct((R, H), BF16),
        ),
        in_specs=[
            SMEM,
            pl.BlockSpec((feat_rows // steps, cw), lambda i: (i, 0)),
            pl.BlockSpec((slot_rows, cw), lambda i: (0, 0)),
            pl.BlockSpec((R // steps, H), lambda i: (i, 0)),
        ],
        out_specs=(
            pl.BlockSpec((feat_rows // steps, cw), lambda i: (i, 0)),
            pl.BlockSpec((R // steps, H), lambda i: (i, 0)),
        ),
        scratch_shapes=[pltpu.VMEM((feat_rows // steps, cw), F32)],
        compiler_params=pltpu.CompilerParams(vmem_limit_bytes=VMEM_BYTES),
        name="finish",
    )(send, base, back, layer_rows)
    return (layer_out, grad_rows)


def solution(mesh):
    return jax.shard_map(
        on_device,
        mesh=mesh,
        in_specs=(
            P(("member", "node"), "feat"),
            P(("member", "node"), None),
            P(("member", "node"), None),
            P("member"),
            P("node"),
            P("node", None, None),
            P("node", None, None),
            P("node", None, None),
            P("node"),
            P(("member", "node", "feat"), None),
        ),
        out_specs=(P(("member", "node", "feat"), None), P(("member", "node"), "feat")),
        check_vma=False,
    )
```

```python
import functools
import math

import jax
import jax.numpy as jnp
from jax import lax
from jax.experimental import pallas as pl
from jax.experimental.pallas import tpu as pltpu
from jax.sharding import PartitionSpec as P

TB = 128
VMEM_BYTES = 60 * 1024 * 1024
F32 = jnp.float32
BF16 = jnp.bfloat16
VMEM = pl.BlockSpec(memory_space=pltpu.VMEM)
SMEM = pl.BlockSpec(memory_space=pltpu.SMEM)
ANY = pl.BlockSpec(memory_space=pl.ANY)


def dot_nn(left, right):
    return lax.dot_general(left, right, (((1,), (0,)), ((), ())), preferred_element_type=F32)


def dot_nt(left, right):
    return lax.dot_general(left, right, (((1,), (1,)), ((), ())), preferred_element_type=F32)


def plan_kernel(n_slot, counts, send, info, edges, features, src_ref, dst_ref, bound_ref, out_blocks, sems):
    per_node, node_count = send.shape
    copies = []
    for peer in range(node_count):
        for s in range(per_node):
            q = peer * per_node + s
            row = pl.multiple_of(send[s, peer] * TB, TB)
            copies.append(
                pltpu.make_async_copy(
                    features.at[pl.ds(row, TB), :],
                    out_blocks.at[pl.ds(q * TB, TB), :],
                    sems.at[q],
                )
            )
    for copy in copies:
        copy.start()
    capacity, edge_slots = edges.shape
    live = counts[0]
    width = bound_ref.shape[1]
    tile = lax.broadcasted_iota(jnp.int32, (1, capacity), 1)
    key = jnp.where(tile < live, info[1] * n_slot + info[0], width).astype(F32)
    total = jnp.where(tile < live, info[2], 0).astype(F32)
    lane = lax.broadcasted_iota(jnp.int32, (capacity, capacity), 1)
    sub = lax.broadcasted_iota(jnp.int32, (capacity, capacity), 0)
    diag = lane == sub

    def column(row):
        return jnp.sum(jnp.where(diag, jnp.broadcast_to(row, diag.shape), 0.0), axis=1, keepdims=True)

    key_col = column(key)
    before = (key_col < key) | ((key_col == key) & (sub < lane))
    rank = jnp.sum(jnp.where(before, 1.0, 0.0), axis=0, keepdims=True)
    order = jnp.where(sub.astype(F32) == rank, 1.0, 0.0).astype(BF16)
    slot_lane = lax.broadcasted_iota(jnp.int32, (capacity, width), 1).astype(F32)
    bound = jnp.sum(jnp.where(key_col < slot_lane, 1.0, 0.0), axis=0, keepdims=True)
    bound_ref[...] = bound.astype(jnp.int32)
    codes = edges[...]
    place = lax.broadcasted_iota(jnp.int32, (capacity, edge_slots), 1).astype(F32)
    source = (codes // TB).astype(F32)
    target = jnp.where(place < column(total), (codes % TB).astype(F32), -1.0)
    src_ref[...] = dot_nn(order, source.astype(BF16))
    dst_ref[...] = dot_nn(order, target.astype(BF16))
    for copy in copies:
        copy.wait()


def final_kernel(send, base, back, layer, grad_ref, layer_ref, rows_sum):
    per_node, node_count = send.shape
    step = pl.program_id(0)
    layer_ref[...] = layer[...]
    rows_sum[...] = base[...].astype(F32)
    blocks = rows_sum.shape[0] // TB
    for peer in range(node_count):
        for s in range(per_node):
            q = peer * per_node + s
            local = send[s, peer] - step * blocks

            @pl.when((local >= 0) & (local < blocks))
            def _():
                rows = pl.ds(pl.multiple_of(local * TB, TB), TB)
                rows_sum[rows, :] += back[q * TB : (q + 1) * TB, :].astype(F32)

    grad_ref[...] = rows_sum[...].astype(BF16)


def main_kernel(
    cfg,
    out_blocks,
    w_self,
    w_neigh,
    bias,
    src_of,
    dst_of,
    bounds,
    features,
    id_row,
    cot,
    layer_ref,
    ret,
    base_ref,
    wbuf,
    wvia,
    prefix,
    adj,
    adj_t,
    scale,
    recv,
    own,
    mean,
    gath,
    g_own,
    g_sum,
    slot_out,
    total,
    sbufs,
    rbufs,
    accs,
    f_send,
    f_recv,
    w_send,
    w_recv,
    h_send,
    h_recv,
    r_send,
    r_recv,
    g_send,
    g_recv,
    b_send,
    b_recv,
    out_sem,
):
    N, F, C, relay, WC = cfg
    L = F.bit_length() - 1
    node = lax.axis_index("node")
    feat = lax.axis_index("feat")
    bits = [(feat // (1 << j)) % 2 for j in range(L)]
    partner = [feat + (1 - 2 * bits[j]) * (1 << j) for j in range(L)]
    rows_all, cw = own.shape
    H = bias.shape[1]
    R = rows_all // F
    RC = R // C
    per = out_blocks.shape[0] // N

    def remote(src, dst, ss, rs, axis, index):
        return pltpu.make_async_remote_copy(
            src_ref=src,
            dst_ref=dst,
            send_sem=ss,
            recv_sem=rs,
            device_id={axis: index},
            device_id_type=pl.DeviceIdType.MESH,
        )

    barrier = pltpu.get_barrier_semaphore()
    for d in range(1, N):
        pl.semaphore_signal(
            barrier, inc=1, device_id={"node": (node + d) % N}, device_id_type=pl.DeviceIdType.MESH
        )
    for j in range(L):
        pl.semaphore_signal(
            barrier, inc=1, device_id={"feat": partner[j]}, device_id_type=pl.DeviceIdType.MESH
        )
    pl.semaphore_wait(barrier, N - 1 + L)

    def node_rows(index):
        return pl.ds(pl.multiple_of(index * per, per), per)

    def exchange(src, dst, ss, rs, d):
        peer = (node + d) % N
        return remote(
            src.at[node_rows(peer), :], dst.at[node_rows(node), :], ss.at[d], rs.at[d], "node", peer
        )

    for d in range(1, N):
        exchange(out_blocks, recv, f_send, f_recv, d).start()
    recv[node_rows(node), :] = out_blocks[node_rows(node), :]

    GC = 2 * WC
    piece = cw // GC
    across = partner[L - 1]
    up, down = (node + 1) % N, (node + N - 1) % N

    def w_rows(c):
        return pl.ds(pl.multiple_of(c * piece, piece), piece)

    def w_copy(c, way, side, peer):
        part = (wbuf.at[0] if way == 0 else wvia).at[w_rows(c), :]
        return remote(part, part, w_send.at[way, side, c], w_recv.at[way, c], "node", peer)

    def hop_copy(c):
        return remote(
            wvia.at[w_rows(c), :], wbuf.at[1, w_rows(c), :], h_send.at[c], h_recv.at[c], "feat", across
        )

    roots = (feat, across)
    go_right = [(node >= r) & (node < N - 1) for r in roots]
    go_left = [(node <= r) & (node > 0) for r in roots]

    def pass_on(c, way, here):
        @pl.when(here & go_right[way])
        def _():
            w_copy(c, way, 0, up).start()

        @pl.when(here & go_left[way])
        def _():
            w_copy(c, way, 1, down).start()

    if relay:

        @pl.when(node == feat)
        def _():
            wbuf[0] = w_self[...]
            wbuf[1] = w_neigh[...]

        @pl.when(node == across)
        def _():
            wvia[...] = w_neigh[...]
        def launch(c, _):
            for way in range(2):
                pass_on(c, way, node == roots[way])
            return 0

        lax.fori_loop(0, GC, launch, 0)
    else:
        wbuf[0] = w_self[...]
        wbuf[1] = w_neigh[...]

    feat_rows = features.shape[0]
    own_step = rows_all // GC
    capacity, edge_slots = src_of.shape
    n_dst = rows_all // TB
    n_slot = recv.shape[0] // TB
    group = capacity // GC
    sub_f = lax.broadcasted_iota(jnp.int32, (TB, edge_slots), 0).astype(BF16)
    one, nil = jnp.ones((), BF16), jnp.zeros((), BF16)
    lane_id = lax.broadcasted_iota(jnp.int32, (TB, TB), 1)
    prefix[0] = jnp.zeros((TB, TB), F32)

    def load(c, _):
        running = prefix[c * group]
        for k in range(group):
            t = c * group + k
            source = jnp.broadcast_to(src_of[pl.ds(t, 1), :].astype(BF16), sub_f.shape)
            target = jnp.broadcast_to(dst_of[pl.ds(t, 1), :].astype(BF16), sub_f.shape)
            t_hot = jnp.where(sub_f == target, one, nil)
            s_hot = jnp.where(sub_f == source, one, nil)
            running = running + dot_nt(t_hot, s_hot)
            prefix[t + 1] = running
        for k in range(own_step // TB):
            rows = pl.ds(pl.multiple_of(c * own_step + k * TB, TB), TB)
            ids = jnp.broadcast_to(id_row[:, rows].astype(F32), (TB, TB)).T.astype(jnp.int32)
            hot = jnp.concatenate(
                [
                    jnp.where(lane_id + b * TB == ids, 1.0, 0.0).astype(BF16)
                    for b in range(feat_rows // TB)
                ],
                axis=1,
            )
            own[rows, :] = dot_nn(hot, features[...]).astype(BF16)
        if relay:

            for way in range(2):

                @pl.when(node != roots[way])
                def _():
                    w_copy(c, way, 0, up).wait_recv()

                pass_on(c, way, node != roots[way])

            @pl.when(node != across)
            def _():
                hop_copy(c).start()

        return 0

    lax.fori_loop(0, GC, load, 0)

    def assemble(b, _):
        rows = pl.ds(pl.multiple_of(b * TB, TB), TB)
        degree = jnp.zeros((TB, TB), F32)
        for s in range(n_slot):
            low, high = bounds[0, b * n_slot + s], bounds[0, b * n_slot + s + 1]
            block = prefix[high] - prefix[low]
            degree = degree + block
            adj[rows, s * TB : (s + 1) * TB] = block.astype(BF16)
            adj_t[s * TB : (s + 1) * TB, rows] = block.T.astype(BF16)
        degree = jnp.sum(degree, axis=1, keepdims=True)
        scale[rows, :] = jnp.broadcast_to(jnp.maximum(degree, 1.0), (TB, TB))
        return 0

    lax.fori_loop(0, n_dst, assemble, 0)

    for d in range(1, N):
        exchange(out_blocks, recv, f_send, f_recv, d).wait_recv()

    def aggregate(i, _):
        rows = pl.ds(pl.multiple_of(i * TB, TB), TB)
        value = dot_nn(adj[rows, :], recv[...]) / scale[rows, :1]
        mean[rows, :] = value.astype(BF16)
        return 0

    lax.fori_loop(0, rows_all // TB, aggregate, 0)

    if relay:

        @pl.when(node != feat)
        def _():
            def landed(c, _):
                hop_copy(c).wait_recv()
                return 0

            lax.fori_loop(0, GC, landed, 0)

    def partial(g, c):
        rows = pl.ds(pl.multiple_of(g * R + c * RC, RC), RC)
        return dot_nn(own[rows, :], wbuf[0]) + dot_nn(mean[rows, :], wbuf[1])

    def r_copy(j, i, c):
        index = sum((F >> (k + 1)) * C for k in range(j)) + i * C + c
        return remote(
            sbufs[j].at[i, c],
            rbufs[j].at[i, c],
            r_send.at[index],
            r_recv.at[index],
            "feat",
            partner[j],
        )

    for c in range(C):
        for i in range(F // 2):
            sbufs[0][i, c] = partial(2 * i + 1 - bits[0], c).astype(BF16)
            r_copy(0, i, c).start()
    for c in range(C):
        for i in range(F // 2):
            accs[0][i, c] = partial(2 * i + bits[0], c)
    for j in range(1, L):
        for c in range(C):
            for a in range(F >> (j + 1)):
                for i in (2 * a, 2 * a + 1):
                    r_copy(j - 1, i, c).wait_recv()
                i = 2 * a + 1 - bits[j]
                sbufs[j][a, c] = (accs[j - 1][i, c] + rbufs[j - 1][i, c].astype(F32)).astype(BF16)
                r_copy(j, a, c).start()
                i = 2 * a + bits[j]
                accs[j][a, c] = accs[j - 1][i, c] + rbufs[j - 1][i, c].astype(F32)

    def g_copy(j, k, c, block):
        index = (j * F + k) * C + c
        part = gath.at[block, c]
        return remote(part, part, g_send.at[index], g_recv.at[index], "feat", partner[j])

    def block_of(mask):
        index = feat
        for j in range(L):
            if mask >> j & 1:
                index = index + (1 - 2 * bits[j]) * (1 << j)
        return index

    def backward(block, c):
        rows = pl.ds(pl.multiple_of(block * R + c * RC, RC), RC)
        rows_grad = gath[block, c]
        g_own[rows, :] = dot_nt(rows_grad, wbuf[0]).astype(BF16)
        to_mean = dot_nt(rows_grad, wbuf[1]).astype(BF16).astype(F32)
        g_sum[rows, :] = (to_mean / scale[rows, :1]).astype(BF16)

    for c in range(C):
        r_copy(L - 1, 0, c).wait_recv()
        pre = accs[L - 1][0, c] + rbufs[L - 1][0, c].astype(F32) + bias[...]
        sig = jax.nn.sigmoid(pre)
        rows = pl.ds(c * RC, RC)
        layer_ref[rows, :] = (pre * sig).astype(BF16)
        gath[feat, c] = (cot[rows, :].astype(F32) * sig * (1.0 + pre * (1.0 - sig))).astype(BF16)
        for j in reversed(range(L)):
            g_copy(j, 0, c, feat).start()
    for c in range(C):
        backward(feat, c)
    for c in range(C):
        for mask in sorted(range(1, F), key=lambda m: (bin(m).count("1"), m)):
            j = (mask & -mask).bit_length() - 1
            g_copy(j, mask >> (j + 1), c, block_of(mask)).wait_recv()
            for low in range(j):
                g_copy(low, mask >> (low + 1), c, block_of(mask)).start()
            backward(block_of(mask), c)

    def slot_grad(peer):
        rows = node_rows(peer)
        slot_out[rows, :] = dot_nn(adj_t[rows, :], g_sum[...]).astype(BF16)

    for d in range(1, N):
        slot_grad((node + d) % N)
        exchange(slot_out, ret, b_send, b_recv, d).start()
    slot_grad(node)
    ret[node_rows(node), :] = slot_out[node_rows(node), :]

    dst_lane = lax.broadcasted_iota(jnp.int32, (TB, rows_all), 0)

    def scatter_own(b, _):
        rows = pl.ds(pl.multiple_of(b * TB, TB), TB)
        hot = jnp.where(dst_lane + b * TB == id_row[...], 1.0, 0.0).astype(BF16)
        total[rows, :] = dot_nn(hot, g_own[...]).astype(BF16)
        return 0

    quarter = feat_rows // 4

    def put(k):
        rows = pl.ds(k * quarter, quarter)
        return pltpu.make_async_copy(total.at[rows, :], base_ref.at[rows, :], out_sem.at[k])

    for k in range(4):
        lax.fori_loop(k * quarter // TB, (k + 1) * quarter // TB, scatter_own, 0)
        put(k).start()
    for d in range(1, N):
        exchange(slot_out, ret, b_send, b_recv, d).wait_recv()
    for k in range(4):
        put(k).wait()

    for d in range(1, N):
        exchange(out_blocks, recv, f_send, f_recv, d).wait_send()
        exchange(slot_out, ret, b_send, b_recv, d).wait_send()
    for j in range(L):
        for c in range(C):
            for i in range(F >> (j + 1)):
                r_copy(j, i, c).wait_send()
            for k in range(F >> (j + 1)):
                g_copy(j, k, c, block_of(k << (j + 1))).wait_send()
    if relay:

        def drain(c, _):
            for way in range(2):

                @pl.when(go_right[way])
                def _():
                    w_copy(c, way, 0, up).wait_send()

                @pl.when(go_left[way])
                def _():
                    w_copy(c, way, 1, down).wait_send()

            @pl.when(node != across)
            def _():
                hop_copy(c).wait_send()

            return 0

        lax.fori_loop(0, GC, drain, 0)


def on_device(
    features,
    w_self,
    w_neigh,
    bias,
    dst_ids,
    send_blocks,
    tile_info,
    tile_edges,
    tile_counts,
    cotangent,
):
    N = lax.axis_size("node")
    F = lax.axis_size("feat")
    L = F.bit_length() - 1
    feat_rows, cw = features.shape
    rows_all = dst_ids.shape[0]
    H = bias.shape[0]
    R = rows_all // F
    C = 2
    WC = 4
    per_node = send_blocks.shape[2]
    slots = N * per_node
    slot_rows = slots * TB
    n_dst = rows_all // TB
    capacity = tile_edges.shape[1]

    send = jnp.swapaxes(send_blocks, 1, 2)[0]
    info = jnp.swapaxes(tile_info, 0, 1)
    width = -(-(n_dst * slots + 1) // TB) * TB
    src_of, dst_of, bounds, out_blocks = pl.pallas_call(
        functools.partial(plan_kernel, slots),
        out_shape=(
            jax.ShapeDtypeStruct(tile_edges.shape[1:], F32),
            jax.ShapeDtypeStruct(tile_edges.shape[1:], F32),
            jax.ShapeDtypeStruct((1, width), jnp.int32),
            jax.ShapeDtypeStruct((slot_rows, cw), BF16),
        ),
        in_specs=[SMEM, SMEM, VMEM, VMEM, ANY],
        out_specs=(VMEM, VMEM, VMEM, VMEM),
        scratch_shapes=[pltpu.SemaphoreType.DMA((slots,))],
        compiler_params=pltpu.CompilerParams(vmem_limit_bytes=VMEM_BYTES),
        name="plan",
    )(tile_counts, send, info, tile_edges[0], features)

    relay = N == F and w_self.shape[0] == cw
    if not relay:
        offset = lax.axis_index("feat") * cw
        w_self, w_neigh = (
            lax.dynamic_slice_in_dim(
                lax.all_gather(w, "node", axis=0, tiled=True), offset, cw, 0
            )
            for w in (w_self, w_neigh)
        )
    dma = pltpu.SemaphoreType.DMA
    halves = [F >> (j + 1) for j in range(L)]
    layer_rows, back, base = pl.pallas_call(
        functools.partial(main_kernel, (N, F, C, relay, WC)),
        out_shape=(
            jax.ShapeDtypeStruct((R, H), BF16),
            jax.ShapeDtypeStruct((slot_rows, cw), BF16),
            jax.ShapeDtypeStruct((feat_rows, cw), BF16),
        ),
        in_specs=[VMEM] * 6 + [SMEM] + [VMEM] * 3,
        out_specs=(VMEM, VMEM, ANY),
        scratch_shapes=[
            pltpu.VMEM((2, cw, H), BF16),
            pltpu.VMEM((cw, H), BF16),
            pltpu.VMEM((capacity + 1, TB, TB), F32),
            pltpu.VMEM((rows_all, slot_rows), BF16),
            pltpu.VMEM((slot_rows, rows_all), BF16),
            pltpu.VMEM((rows_all, TB), F32),
            pltpu.VMEM((slot_rows, cw), BF16),
            pltpu.VMEM((rows_all, cw), BF16),
            pltpu.VMEM((rows_all, cw), BF16),
            pltpu.VMEM((F, C, R // C, H), BF16),
            pltpu.VMEM((rows_all, cw), BF16),
            pltpu.VMEM((rows_all, cw), BF16),
            pltpu.VMEM((slot_rows, cw), BF16),
            pltpu.VMEM((feat_rows, cw), BF16),
            [pltpu.VMEM((h, C, R // C, H), BF16) for h in halves],
            [pltpu.VMEM((h, C, R // C, H), BF16) for h in halves],
            [pltpu.VMEM((h, C, R // C, H), F32) for h in halves],
            dma((N,)),
            dma((N,)),
            dma((2, 2, 2 * WC)),
            dma((2, 2 * WC)),
            dma((2 * WC,)),
            dma((2 * WC,)),
            dma((F * C,)),
            dma((F * C,)),
            dma((L * F * C,)),
            dma((L * F * C,)),
            dma((N,)),
            dma((N,)),
            dma((4,)),
        ],
        compiler_params=pltpu.CompilerParams(
            collective_id=0, has_side_effects=True, vmem_limit_bytes=VMEM_BYTES
        ),
        name="layer",
    )(
        out_blocks,
        w_self,
        w_neigh,
        bias.reshape(1, H),
        src_of,
        dst_of,
        bounds,
        features,
        dst_ids.reshape(1, -1),
        cotangent,
    )
    steps = math.gcd(math.gcd(feat_rows // TB, R // 16), 2)
    grad_rows, layer_out = pl.pallas_call(
        final_kernel,
        grid=(steps,),
        out_shape=(
            jax.ShapeDtypeStruct((feat_rows, cw), BF16),
            jax.ShapeDtypeStruct((R, H), BF16),
        ),
        in_specs=[
            SMEM,
            pl.BlockSpec((feat_rows // steps, cw), lambda i: (i, 0)),
            pl.BlockSpec((slot_rows, cw), lambda i: (0, 0)),
            pl.BlockSpec((R // steps, H), lambda i: (i, 0)),
        ],
        out_specs=(
            pl.BlockSpec((feat_rows // steps, cw), lambda i: (i, 0)),
            pl.BlockSpec((R // steps, H), lambda i: (i, 0)),
        ),
        scratch_shapes=[pltpu.VMEM((feat_rows // steps, cw), F32)],
        compiler_params=pltpu.CompilerParams(vmem_limit_bytes=VMEM_BYTES),
        name="finish",
    )(send, base, back, layer_rows)
    return (layer_out, grad_rows)


def solution(mesh):
    return jax.shard_map(
        on_device,
        mesh=mesh,
        in_specs=(
            P(("member", "node"), "feat"),
            P(("member", "node"), None),
            P(("member", "node"), None),
            P("member"),
            P("node"),
            P("node", None, None),
            P("node", None, None),
            P("node", None, None),
            P("node"),
            P(("member", "node", "feat"), None),
        ),
        out_specs=(P(("member", "node", "feat"), None), P(("member", "node"), "feat")),
        check_vma=False,
    )
```

```python
import functools
import math

import jax
import jax.numpy as jnp
from jax import lax
from jax.experimental import pallas as pl
from jax.experimental.pallas import tpu as pltpu
from jax.sharding import PartitionSpec as P

TB = 128
VMEM_BYTES = 60 * 1024 * 1024
F32 = jnp.float32
BF16 = jnp.bfloat16
VMEM = pl.BlockSpec(memory_space=pltpu.VMEM)
SMEM = pl.BlockSpec(memory_space=pltpu.SMEM)
ANY = pl.BlockSpec(memory_space=pl.ANY)


def dot_nn(left, right):
    return lax.dot_general(left, right, (((1,), (0,)), ((), ())), preferred_element_type=F32)


def dot_nt(left, right):
    return lax.dot_general(left, right, (((1,), (1,)), ((), ())), preferred_element_type=F32)


def plan_kernel(n_slot, counts, send, info, edges, features, src_ref, dst_ref, bound_ref, out_blocks, sems):
    per_node, node_count = send.shape
    copies = []
    for peer in range(node_count):
        for s in range(per_node):
            q = peer * per_node + s
            row = pl.multiple_of(send[s, peer] * TB, TB)
            copies.append(
                pltpu.make_async_copy(
                    features.at[pl.ds(row, TB), :],
                    out_blocks.at[pl.ds(q * TB, TB), :],
                    sems.at[q],
                )
            )
    for copy in copies:
        copy.start()
    capacity, edge_slots = edges.shape
    live = counts[0]
    width = bound_ref.shape[1]
    tile = lax.broadcasted_iota(jnp.int32, (1, capacity), 1)
    key = jnp.where(tile < live, info[1] * n_slot + info[0], width).astype(F32)
    total = jnp.where(tile < live, info[2], 0).astype(F32)
    lane = lax.broadcasted_iota(jnp.int32, (capacity, capacity), 1)
    sub = lax.broadcasted_iota(jnp.int32, (capacity, capacity), 0)
    diag = lane == sub

    def column(row):
        return jnp.sum(jnp.where(diag, jnp.broadcast_to(row, diag.shape), 0.0), axis=1, keepdims=True)

    key_col = column(key)
    before = (key_col < key) | ((key_col == key) & (sub < lane))
    rank = jnp.sum(jnp.where(before, 1.0, 0.0), axis=0, keepdims=True)
    order = jnp.where(sub.astype(F32) == rank, 1.0, 0.0).astype(BF16)
    slot_lane = lax.broadcasted_iota(jnp.int32, (capacity, width), 1).astype(F32)
    bound = jnp.sum(jnp.where(key_col < slot_lane, 1.0, 0.0), axis=0, keepdims=True)
    bound_ref[...] = bound.astype(jnp.int32)
    codes = edges[...]
    place = lax.broadcasted_iota(jnp.int32, (capacity, edge_slots), 1).astype(F32)
    source = (codes // TB).astype(F32)
    target = jnp.where(place < column(total), (codes % TB).astype(F32), -1.0)
    src_ref[...] = dot_nn(order, source.astype(BF16))
    dst_ref[...] = dot_nn(order, target.astype(BF16))
    for copy in copies:
        copy.wait()


def final_kernel(send, base, back, layer, grad_ref, layer_ref, rows_sum):
    per_node, node_count = send.shape
    step = pl.program_id(0)
    layer_ref[...] = layer[...]
    rows_sum[...] = base[...].astype(F32)
    blocks = rows_sum.shape[0] // TB
    for peer in range(node_count):
        for s in range(per_node):
            q = peer * per_node + s
            local = send[s, peer] - step * blocks

            @pl.when((local >= 0) & (local < blocks))
            def _():
                rows = pl.ds(pl.multiple_of(local * TB, TB), TB)
                rows_sum[rows, :] += back[q * TB : (q + 1) * TB, :].astype(F32)

    grad_ref[...] = rows_sum[...].astype(BF16)


def main_kernel(
    cfg,
    out_blocks,
    w_self,
    w_neigh,
    bias,
    src_of,
    dst_of,
    bounds,
    features,
    id_row,
    cot,
    layer_ref,
    ret,
    base_ref,
    wbuf,
    wvia,
    prefix,
    adj,
    adj_t,
    scale,
    recv,
    own,
    mean,
    gath,
    g_own,
    g_sum,
    slot_out,
    total,
    sbufs,
    rbufs,
    accs,
    f_send,
    f_recv,
    w_send,
    w_recv,
    h_send,
    h_recv,
    r_send,
    r_recv,
    g_send,
    g_recv,
    b_send,
    b_recv,
    out_sem,
):
    N, F, C, relay, WC = cfg
    L = F.bit_length() - 1
    node = lax.axis_index("node")
    feat = lax.axis_index("feat")
    bits = [(feat // (1 << j)) % 2 for j in range(L)]
    partner = [feat + (1 - 2 * bits[j]) * (1 << j) for j in range(L)]
    rows_all, cw = own.shape
    H = bias.shape[1]
    R = rows_all // F
    RC = R // C
    per = out_blocks.shape[0] // N

    def remote(src, dst, ss, rs, axis, index):
        return pltpu.make_async_remote_copy(
            src_ref=src,
            dst_ref=dst,
            send_sem=ss,
            recv_sem=rs,
            device_id={axis: index},
            device_id_type=pl.DeviceIdType.MESH,
        )

    barrier = pltpu.get_barrier_semaphore()
    for d in range(1, N):
        pl.semaphore_signal(
            barrier, inc=1, device_id={"node": (node + d) % N}, device_id_type=pl.DeviceIdType.MESH
        )
    for j in range(L):
        pl.semaphore_signal(
            barrier, inc=1, device_id={"feat": partner[j]}, device_id_type=pl.DeviceIdType.MESH
        )
    pl.semaphore_wait(barrier, N - 1 + L)

    def node_rows(index):
        return pl.ds(pl.multiple_of(index * per, per), per)

    def exchange(src, dst, ss, rs, d):
        peer = (node + d) % N
        return remote(
            src.at[node_rows(peer), :], dst.at[node_rows(node), :], ss.at[d], rs.at[d], "node", peer
        )

    for d in range(1, N):
        exchange(out_blocks, recv, f_send, f_recv, d).start()
    recv[node_rows(node), :] = out_blocks[node_rows(node), :]

    GC = 2 * WC
    piece = cw // GC
    across = partner[L - 1]
    up, down = (node + 1) % N, (node + N - 1) % N

    def w_rows(c):
        return pl.ds(pl.multiple_of(c * piece, piece), piece)

    def w_copy(c, way, side, peer):
        part = (wbuf.at[0] if way == 0 else wvia).at[w_rows(c), :]
        return remote(part, part, w_send.at[way, side, c], w_recv.at[way, c], "node", peer)

    def hop_copy(c):
        return remote(
            wvia.at[w_rows(c), :], wbuf.at[1, w_rows(c), :], h_send.at[c], h_recv.at[c], "feat", across
        )

    roots = (feat, across)
    go_right = [(node >= r) & (node < N - 1) for r in roots]
    go_left = [(node <= r) & (node > 0) for r in roots]

    def pass_on(c, way, here):
        @pl.when(here & go_right[way])
        def _():
            w_copy(c, way, 0, up).start()

        @pl.when(here & go_left[way])
        def _():
            w_copy(c, way, 1, down).start()

    if relay:

        @pl.when(node == feat)
        def _():
            wbuf[0] = w_self[...]
            wbuf[1] = w_neigh[...]

        @pl.when(node == across)
        def _():
            wvia[...] = w_neigh[...]
        def launch(c, _):
            for way in range(2):
                pass_on(c, way, node == roots[way])
            return 0

        lax.fori_loop(0, GC, launch, 0)
    else:
        wbuf[0] = w_self[...]
        wbuf[1] = w_neigh[...]

    feat_rows = features.shape[0]
    own_step = rows_all // GC
    capacity, edge_slots = src_of.shape
    n_dst = rows_all // TB
    n_slot = recv.shape[0] // TB
    group = capacity // GC
    sub_f = lax.broadcasted_iota(jnp.int32, (TB, edge_slots), 0).astype(BF16)
    one, nil = jnp.ones((), BF16), jnp.zeros((), BF16)
    lane_id = lax.broadcasted_iota(jnp.int32, (TB, TB), 1)
    prefix[0] = jnp.zeros((TB, TB), F32)

    def relay_piece(c):
        for way in range(2):

            @pl.when(node != roots[way])
            def _():
                w_copy(c, way, 0, up).wait_recv()

            pass_on(c, way, node != roots[way])

        @pl.when(node != across)
        def _():
            hop_copy(c).start()

    def load(c, _):
        running = prefix[c * group]
        for k in range(group):
            t = c * group + k
            source = jnp.broadcast_to(src_of[pl.ds(t, 1), :].astype(BF16), sub_f.shape)
            target = jnp.broadcast_to(dst_of[pl.ds(t, 1), :].astype(BF16), sub_f.shape)
            t_hot = jnp.where(sub_f == target, one, nil)
            s_hot = jnp.where(sub_f == source, one, nil)
            running = running + dot_nt(t_hot, s_hot)
            prefix[t + 1] = running
        for k in range(own_step // TB):
            rows = pl.ds(pl.multiple_of(c * own_step + k * TB, TB), TB)
            ids = jnp.broadcast_to(id_row[:, rows].astype(F32), (TB, TB)).T.astype(jnp.int32)
            hot = jnp.concatenate(
                [
                    jnp.where(lane_id + b * TB == ids, 1.0, 0.0).astype(BF16)
                    for b in range(feat_rows // TB)
                ],
                axis=1,
            )
            own[rows, :] = dot_nn(hot, features[...]).astype(BF16)
        if relay:

            @pl.when(c >= WC)
            def _():
                relay_piece(c - WC)

        return 0

    lax.fori_loop(0, GC, load, 0)

    def assemble(b, _):
        rows = pl.ds(pl.multiple_of(b * TB, TB), TB)
        degree = jnp.zeros((TB, TB), F32)
        for s in range(n_slot):
            low, high = bounds[0, b * n_slot + s], bounds[0, b * n_slot + s + 1]
            block = prefix[high] - prefix[low]
            degree = degree + block
            adj[rows, s * TB : (s + 1) * TB] = block.astype(BF16)
            adj_t[s * TB : (s + 1) * TB, rows] = block.T.astype(BF16)
        degree = jnp.sum(degree, axis=1, keepdims=True)
        scale[rows, :] = jnp.broadcast_to(jnp.maximum(degree, 1.0), (TB, TB))
        return 0

    lax.fori_loop(0, n_dst, assemble, 0)
    if relay:
        relay_piece(WC)

    for d in range(1, N):
        exchange(out_blocks, recv, f_send, f_recv, d).wait_recv()

    def aggregate(i, _):
        rows = pl.ds(pl.multiple_of(i * TB, TB), TB)
        value = dot_nn(adj[rows, :], recv[...]) / scale[rows, :1]
        mean[rows, :] = value.astype(BF16)
        return 0

    lax.fori_loop(0, rows_all // TB, aggregate, 0)
    if relay:

        def rest(c, _):
            relay_piece(c)
            return 0

        lax.fori_loop(WC + 1, GC, rest, 0)

    if relay:

        @pl.when(node != feat)
        def _():
            def landed(c, _):
                hop_copy(c).wait_recv()
                return 0

            lax.fori_loop(0, GC, landed, 0)

    def partial(g, c):
        rows = pl.ds(pl.multiple_of(g * R + c * RC, RC), RC)
        return dot_nn(own[rows, :], wbuf[0]) + dot_nn(mean[rows, :], wbuf[1])

    def r_copy(j, i, c):
        index = sum((F >> (k + 1)) * C for k in range(j)) + i * C + c
        return remote(
            sbufs[j].at[i, c],
            rbufs[j].at[i, c],
            r_send.at[index],
            r_recv.at[index],
            "feat",
            partner[j],
        )

    for c in range(C):
        for i in range(F // 2):
            sbufs[0][i, c] = partial(2 * i + 1 - bits[0], c).astype(BF16)
            r_copy(0, i, c).start()
    for c in range(C):
        for i in range(F // 2):
            accs[0][i, c] = partial(2 * i + bits[0], c)
    for j in range(1, L):
        for c in range(C):
            for a in range(F >> (j + 1)):
                for i in (2 * a, 2 * a + 1):
                    r_copy(j - 1, i, c).wait_recv()
                i = 2 * a + 1 - bits[j]
                sbufs[j][a, c] = (accs[j - 1][i, c] + rbufs[j - 1][i, c].astype(F32)).astype(BF16)
                r_copy(j, a, c).start()
                i = 2 * a + bits[j]
                accs[j][a, c] = accs[j - 1][i, c] + rbufs[j - 1][i, c].astype(F32)

    def g_copy(j, k, c, block):
        index = (j * F + k) * C + c
        part = gath.at[block, c]
        return remote(part, part, g_send.at[index], g_recv.at[index], "feat", partner[j])

    def block_of(mask):
        index = feat
        for j in range(L):
            if mask >> j & 1:
                index = index + (1 - 2 * bits[j]) * (1 << j)
        return index

    def backward(block, c):
        rows = pl.ds(pl.multiple_of(block * R + c * RC, RC), RC)
        rows_grad = gath[block, c]
        g_own[rows, :] = dot_nt(rows_grad, wbuf[0]).astype(BF16)
        to_mean = dot_nt(rows_grad, wbuf[1]).astype(BF16).astype(F32)
        g_sum[rows, :] = (to_mean / scale[rows, :1]).astype(BF16)

    for c in range(C):
        r_copy(L - 1, 0, c).wait_recv()
        pre = accs[L - 1][0, c] + rbufs[L - 1][0, c].astype(F32) + bias[...]
        sig = jax.nn.sigmoid(pre)
        rows = pl.ds(c * RC, RC)
        layer_ref[rows, :] = (pre * sig).astype(BF16)
        gath[feat, c] = (cot[rows, :].astype(F32) * sig * (1.0 + pre * (1.0 - sig))).astype(BF16)
        for j in reversed(range(L)):
            g_copy(j, 0, c, feat).start()
    for c in range(C):
        backward(feat, c)
    for c in range(C):
        for mask in sorted(range(1, F), key=lambda m: (bin(m).count("1"), m)):
            j = (mask & -mask).bit_length() - 1
            g_copy(j, mask >> (j + 1), c, block_of(mask)).wait_recv()
            for low in range(j):
                g_copy(low, mask >> (low + 1), c, block_of(mask)).start()
            backward(block_of(mask), c)

    def slot_grad(peer):
        rows = node_rows(peer)
        slot_out[rows, :] = dot_nn(adj_t[rows, :], g_sum[...]).astype(BF16)

    for d in range(1, N):
        slot_grad((node + d) % N)
        exchange(slot_out, ret, b_send, b_recv, d).start()
    slot_grad(node)
    ret[node_rows(node), :] = slot_out[node_rows(node), :]

    dst_lane = lax.broadcasted_iota(jnp.int32, (TB, rows_all), 0)

    def scatter_own(b, _):
        rows = pl.ds(pl.multiple_of(b * TB, TB), TB)
        hot = jnp.where(dst_lane + b * TB == id_row[...], 1.0, 0.0).astype(BF16)
        total[rows, :] = dot_nn(hot, g_own[...]).astype(BF16)
        return 0

    quarter = feat_rows // 4

    def put(k):
        rows = pl.ds(k * quarter, quarter)
        return pltpu.make_async_copy(total.at[rows, :], base_ref.at[rows, :], out_sem.at[k])

    for k in range(4):
        lax.fori_loop(k * quarter // TB, (k + 1) * quarter // TB, scatter_own, 0)
        put(k).start()
    for d in range(1, N):
        exchange(slot_out, ret, b_send, b_recv, d).wait_recv()
    for k in range(4):
        put(k).wait()

    for d in range(1, N):
        exchange(out_blocks, recv, f_send, f_recv, d).wait_send()
        exchange(slot_out, ret, b_send, b_recv, d).wait_send()
    for j in range(L):
        for c in range(C):
            for i in range(F >> (j + 1)):
                r_copy(j, i, c).wait_send()
            for k in range(F >> (j + 1)):
                g_copy(j, k, c, block_of(k << (j + 1))).wait_send()
    if relay:

        def drain(c, _):
            for way in range(2):

                @pl.when(go_right[way])
                def _():
                    w_copy(c, way, 0, up).wait_send()

                @pl.when(go_left[way])
                def _():
                    w_copy(c, way, 1, down).wait_send()

            @pl.when(node != across)
            def _():
                hop_copy(c).wait_send()

            return 0

        lax.fori_loop(0, GC, drain, 0)


def on_device(
    features,
    w_self,
    w_neigh,
    bias,
    dst_ids,
    send_blocks,
    tile_info,
    tile_edges,
    tile_counts,
    cotangent,
):
    N = lax.axis_size("node")
    F = lax.axis_size("feat")
    L = F.bit_length() - 1
    feat_rows, cw = features.shape
    rows_all = dst_ids.shape[0]
    H = bias.shape[0]
    R = rows_all // F
    C = 2
    WC = 4
    per_node = send_blocks.shape[2]
    slots = N * per_node
    slot_rows = slots * TB
    n_dst = rows_all // TB
    capacity = tile_edges.shape[1]

    send = jnp.swapaxes(send_blocks, 1, 2)[0]
    info = jnp.swapaxes(tile_info, 0, 1)
    width = -(-(n_dst * slots + 1) // TB) * TB
    src_of, dst_of, bounds, out_blocks = pl.pallas_call(
        functools.partial(plan_kernel, slots),
        out_shape=(
            jax.ShapeDtypeStruct(tile_edges.shape[1:], F32),
            jax.ShapeDtypeStruct(tile_edges.shape[1:], F32),
            jax.ShapeDtypeStruct((1, width), jnp.int32),
            jax.ShapeDtypeStruct((slot_rows, cw), BF16),
        ),
        in_specs=[SMEM, SMEM, VMEM, VMEM, ANY],
        out_specs=(VMEM, VMEM, VMEM, VMEM),
        scratch_shapes=[pltpu.SemaphoreType.DMA((slots,))],
        compiler_params=pltpu.CompilerParams(vmem_limit_bytes=VMEM_BYTES),
        name="plan",
    )(tile_counts, send, info, tile_edges[0], features)

    relay = N == F and w_self.shape[0] == cw
    if not relay:
        offset = lax.axis_index("feat") * cw
        w_self, w_neigh = (
            lax.dynamic_slice_in_dim(
                lax.all_gather(w, "node", axis=0, tiled=True), offset, cw, 0
            )
            for w in (w_self, w_neigh)
        )
    dma = pltpu.SemaphoreType.DMA
    halves = [F >> (j + 1) for j in range(L)]
    layer_rows, back, base = pl.pallas_call(
        functools.partial(main_kernel, (N, F, C, relay, WC)),
        out_shape=(
            jax.ShapeDtypeStruct((R, H), BF16),
            jax.ShapeDtypeStruct((slot_rows, cw), BF16),
            jax.ShapeDtypeStruct((feat_rows, cw), BF16),
        ),
        in_specs=[VMEM] * 6 + [SMEM] + [VMEM] * 3,
        out_specs=(VMEM, VMEM, ANY),
        scratch_shapes=[
            pltpu.VMEM((2, cw, H), BF16),
            pltpu.VMEM((cw, H), BF16),
            pltpu.VMEM((capacity + 1, TB, TB), F32),
            pltpu.VMEM((rows_all, slot_rows), BF16),
            pltpu.VMEM((slot_rows, rows_all), BF16),
            pltpu.VMEM((rows_all, TB), F32),
            pltpu.VMEM((slot_rows, cw), BF16),
            pltpu.VMEM((rows_all, cw), BF16),
            pltpu.VMEM((rows_all, cw), BF16),
            pltpu.VMEM((F, C, R // C, H), BF16),
            pltpu.VMEM((rows_all, cw), BF16),
            pltpu.VMEM((rows_all, cw), BF16),
            pltpu.VMEM((slot_rows, cw), BF16),
            pltpu.VMEM((feat_rows, cw), BF16),
            [pltpu.VMEM((h, C, R // C, H), BF16) for h in halves],
            [pltpu.VMEM((h, C, R // C, H), BF16) for h in halves],
            [pltpu.VMEM((h, C, R // C, H), F32) for h in halves],
            dma((N,)),
            dma((N,)),
            dma((2, 2, 2 * WC)),
            dma((2, 2 * WC)),
            dma((2 * WC,)),
            dma((2 * WC,)),
            dma((F * C,)),
            dma((F * C,)),
            dma((L * F * C,)),
            dma((L * F * C,)),
            dma((N,)),
            dma((N,)),
            dma((4,)),
        ],
        compiler_params=pltpu.CompilerParams(
            collective_id=0, has_side_effects=True, vmem_limit_bytes=VMEM_BYTES
        ),
        name="layer",
    )(
        out_blocks,
        w_self,
        w_neigh,
        bias.reshape(1, H),
        src_of,
        dst_of,
        bounds,
        features,
        dst_ids.reshape(1, -1),
        cotangent,
    )
    steps = math.gcd(math.gcd(feat_rows // TB, R // 16), 2)
    grad_rows, layer_out = pl.pallas_call(
        final_kernel,
        grid=(steps,),
        out_shape=(
            jax.ShapeDtypeStruct((feat_rows, cw), BF16),
            jax.ShapeDtypeStruct((R, H), BF16),
        ),
        in_specs=[
            SMEM,
            pl.BlockSpec((feat_rows // steps, cw), lambda i: (i, 0)),
            pl.BlockSpec((slot_rows, cw), lambda i: (0, 0)),
            pl.BlockSpec((R // steps, H), lambda i: (i, 0)),
        ],
        out_specs=(
            pl.BlockSpec((feat_rows // steps, cw), lambda i: (i, 0)),
            pl.BlockSpec((R // steps, H), lambda i: (i, 0)),
        ),
        scratch_shapes=[pltpu.VMEM((feat_rows // steps, cw), F32)],
        compiler_params=pltpu.CompilerParams(vmem_limit_bytes=VMEM_BYTES),
        name="finish",
    )(send, base, back, layer_rows)
    return (layer_out, grad_rows)


def solution(mesh):
    return jax.shard_map(
        on_device,
        mesh=mesh,
        in_specs=(
            P(("member", "node"), "feat"),
            P(("member", "node"), None),
            P(("member", "node"), None),
            P("member"),
            P("node"),
            P("node", None, None),
            P("node", None, None),
            P("node", None, None),
            P("node"),
            P(("member", "node", "feat"), None),
        ),
        out_specs=(P(("member", "node", "feat"), None), P(("member", "node"), "feat")),
        check_vma=False,
    )
```
